256 devices in a mesh: tm: 32 (over y, z_hi, core), height: 4 (over x), head: 2 (over z_lo).
Axes of the slice: x: 4, y: 4, z: 8 (z_hi: 4, z_lo: 2; z = z_hi * 2 + z_lo), core: 2. Of those that a mesh axis runs over, the one named last changes fastest.
Arguments:
- queries: bfloat16 [65536, 1536], P(('tm', 'height'), 'head'), may hold values from -5 to 5
- keys: bfloat16 [65536, 1536], P(('tm', 'height'), 'head'), may hold values from -5 to 5
- values: bfloat16 [65536, 1536], P(('tm', 'height'), 'head'), may hold values from -6 to 6
- out_weight: bfloat16 [1536, 3072], P('head'), may hold values from -0.15625 to 0.15625
- kv_list: int32 [128, 8], P(('tm', 'height')), may hold values from 0 to 127, as said below
- kv_count: int32 [128], P(('tm', 'height')), may hold values from 1 to 8, as said below
Outputs:
- mixed: bfloat16 [65536, 3072], P(('tm', 'height'), 'head')
The draws below stay inside these ranges and needn't reach their ends.
Inputs may be any that keep to these rules, and one draw needn't show every extreme that they name: Entries of kv_list[b] at positions below kv_count[b] are distinct; the first is b; each other is one frame away in the same band (b + 4 or b - 4), one band away in the same frame (b + 1 or b - 1 within the frame), or in the same band at a frame distance that is a power of two from 2 to below 32. Entries at later positions equal b. `kv_count`: number of listed key blocks; some block has 8.
All inputs are finite; a program needn't handle non-finite values.
Results may differ from the reference program's by a relative error of at most 0.015.
Values may be sent and summed in bfloat16 or wider, within the bound.
A program may use at most 192 MiB of HBM per device.

```python
import jax
import jax.numpy as jnp
from jax import lax

D = 3072
HEADS = 12
HEAD_DIM = 128
TOK_DEV = 512
FRAMES = 32
BANDS = 4
BLOCKS = 128
TOKENS = 65536
HD = 1536
MOST = 8


def draw_queries(key, part):
    key = jax.random.fold_in(key, 1)
    drawn_draw = jnp.clip(jax.random.normal(key, (TOKENS, HD), jnp.float32), -4.5, 4.5)
    return drawn_draw.astype(jnp.bfloat16)


def draw_keys(key, part):
    key = jax.random.fold_in(key, 2)
    drawn_draw = jnp.clip(jax.random.normal(key, (TOKENS, HD), jnp.float32), -4.5, 4.5)
    return drawn_draw.astype(jnp.bfloat16)


def radial_lists(key):
    offsets = [(0, 0), (-1, 0), (1, 0), (0, -1), (0, 1)]
    distance = 2
    while distance < FRAMES:
        offsets = offsets + [(distance, 0), (-distance, 0)]
        distance = distance * 2
    width_count = len(offsets)
    frame_steps = jnp.array([pair_item[0] for pair_item in offsets], dtype=jnp.int32)
    band_steps = jnp.array([pair_item[1] for pair_item in offsets], dtype=jnp.int32)
    block_ids = jnp.arange(BLOCKS, dtype=jnp.int32)
    frame_to = (block_ids // BANDS)[:, None] + frame_steps[None, :]
    band_to = (block_ids % BANDS)[:, None] + band_steps[None, :]
    usable = (frame_to >= 0) & (frame_to < FRAMES) & (band_to >= 0) & (band_to < BANDS)
    target_ids = frame_to * BANDS + band_to
    columns = jnp.arange(width_count, dtype=jnp.int32)[None, :]
    noise = jax.random.randint(jax.random.fold_in(key, 21), (BLOCKS, width_count), 0, 1000)
    priority = noise * 64 + columns
    priority = jnp.where(columns == 0, -1, priority)
    priority = jnp.where(usable, priority, 100000000)
    order = jnp.argsort(priority, axis=1, stable=True)
    sorted_ids = jnp.take_along_axis(target_ids, order, axis=1)[:, :MOST]
    available = jnp.sum(usable.astype(jnp.int32), axis=1)
    wanted = jax.random.randint(jax.random.fold_in(key, 22), (BLOCKS,), MOST - 2, MOST + 1)
    counts = jnp.minimum(available, wanted)
    pick_frame = FRAMES // 2
    pick_band = jax.random.randint(jax.random.fold_in(key, 24), (), 1, BANDS - 1)
    counts = jnp.where(block_ids == pick_frame * BANDS + pick_band, MOST, counts)
    positions = jnp.arange(MOST, dtype=jnp.int32)[None, :]
    lists = jnp.where(positions < counts[:, None], sorted_ids, block_ids[:, None])
    return (lists.astype(jnp.int32), counts.astype(jnp.int32))


def draw_kv_list(key, part):
    lists, counts = radial_lists(key)
    return lists


def draw_kv_count(key, part):
    lists, counts = radial_lists(key)
    return counts


def block_scale(key, dims, shards, least, top_value):
    def one(axis_at, blocks):
        steps = jax.random.uniform(jax.random.fold_in(jax.random.fold_in(key, 6), axis_at), (blocks,), jnp.float32, least / len(shards), top_value / len(shards))
        return jnp.repeat(jnp.exp(steps), dims[axis_at] // blocks).reshape((-1,) + (1,) * (len(dims) - axis_at - 1))

    level = one(*shards[0])
    for cut in shards[1:]:
        level = level * one(*cut)
    return level


def normal_values(key, shape, width, limit, pieces=(), kind=jnp.bfloat16):
    loudness = block_scale(key, shape, pieces, -0.22, 0.18) if pieces else 1.0
    drawn = jax.random.normal(key, shape, jnp.float32) * width * loudness
    return jnp.minimum(jnp.maximum(drawn, -limit), limit).astype(kind)


def setup_inputs(seed: int = 0) -> dict:
    key_list = jax.random.split(jax.random.key(seed), 7)
    queries = draw_queries(jax.random.fold_in(key_list[6], 71), 0)
    keys = draw_keys(jax.random.fold_in(key_list[6], 71), 0)
    values = normal_values(key_list[2], (TOKENS, HD), 1.0, 6.0, ((0, 128), (1, 2)))
    out_weight = normal_values(key_list[3], (HD, D), HD ** -0.5, 0.15625, ((0, 2),))
    kv_list = draw_kv_list(jax.random.fold_in(key_list[6], 71), 0)
    kv_count = draw_kv_count(jax.random.fold_in(key_list[6], 71), 0)
    return dict(queries=queries, keys=keys, values=values, out_weight=out_weight, kv_list=kv_list, kv_count=kv_count)


def reference(queries, keys, values, out_weight, kv_list, kv_count):
    score_scale = HEAD_DIM ** -0.5
    query_blocks = queries.reshape(BLOCKS, TOK_DEV, HEADS, HEAD_DIM)
    key_blocks = keys.reshape(BLOCKS, TOK_DEV, HEADS, HEAD_DIM)
    value_blocks = values.reshape(BLOCKS, TOK_DEV, HEADS, HEAD_DIM)

    def attend_block(block):
        block_ids = kv_list[block].astype(jnp.int32)
        listed_count = kv_count[block]
        key_rows = key_blocks[block_ids].reshape(MOST * TOK_DEV, HEADS, HEAD_DIM).astype(jnp.float32)
        value_rows = value_blocks[block_ids].reshape(MOST * TOK_DEV, HEADS, HEAD_DIM).astype(jnp.float32)
        query_rows = query_blocks[block].astype(jnp.float32)
        scores = jnp.einsum("qhd,khd->hqk", query_rows, key_rows) * score_scale
        alive = jnp.repeat(jnp.arange(MOST, dtype=jnp.int32) < listed_count, TOK_DEV)
        scores = jnp.where(alive[None, None, :], scores, jnp.float32(-1e30))
        largest = jnp.max(scores, axis=-1, keepdims=True)
        weights = jnp.exp(scores - largest)
        totals = jnp.sum(weights, axis=-1)
        rounded = lax.optimization_barrier(weights.astype(jnp.bfloat16)).astype(jnp.float32)
        weighted = jnp.einsum("hqk,khd->qhd", rounded, value_rows)
        attended = weighted / jnp.transpose(totals)[:, :, None]
        return attended.reshape(TOK_DEV, HD).astype(jnp.bfloat16)

    attended = lax.map(attend_block, jnp.arange(BLOCKS, dtype=jnp.int32)).reshape(TOKENS, HD)
    return jnp.dot(attended, out_weight, preferred_element_type=jnp.float32).astype(jnp.bfloat16)
```

```python
import functools

import jax
import jax.numpy as jnp
from jax import lax
from jax.experimental import pallas as pl
from jax.experimental.pallas import tpu as pltpu
from jax.sharding import PartitionSpec as P

HEAD_DIM = 128
SIDE = 4
SCORE_SCALE = HEAD_DIM ** (-0.5) * 1.4426950408889634
UNLISTED = -1e30
ROWS = 128
AHEAD = 2

OWN, OTHER, XLO, XHI, YLO, YHI, ZHI, ZLO, ZOP, EDGE1, YOP, NEAR, EDGE2 = range(13)
SLOTS = 13

(TO_ZUP, TO_ZDOWN, RELAY_ZUP, RELAY_ZDOWN, TO_YDOWN, RELAY_YDOWN, TO_YUP, TO_EDGE1,
 TO_EDGE2, TO_XDOWN, TO_XUP, TO_CORE, TO_NEAR, TO_HEAD) = range(14)
SENDS = 14


def kernel(heads, kv_list, kv_count, q_ref, k_hbm, v_hbm, w_hbm, out_ref,
           kv, att, wbuf, total, top, sums, acc,
           send, recv, recv_v, att_recv, load, wload, wsend, wrecv):
    tm = lax.axis_index("tm")
    x = lax.axis_index("height")
    part = lax.axis_index("head")
    core = lax.rem(tm, 2)
    chip = lax.div(tm, 2)
    z = lax.rem(chip, SIDE)
    y = lax.div(chip, SIDE)
    far = lax.div(z, 2)
    sign = 1 - 2 * far
    ym = y * (1 - far) + (SIDE - 1 - y) * far
    zm = z * (1 - far) + (SIDE - 1 - z) * far

    def at(yy, zz, cc):
        return (yy * SIDE + zz) * 2 + cc

    zup, zdown = lax.rem(z + 1, SIDE), lax.rem(z + 3, SIDE)
    yup, ydown = lax.rem(y + sign + SIDE, SIDE), lax.rem(y - sign + SIDE, SIDE)
    dev_zup = (at(y, zup, core), x, part)
    dev_zdown = (at(y, zdown, core), x, part)
    dev_yup = (at(yup, z, core), x, part)
    dev_ydown = (at(ydown, z, core), x, part)
    dev_core = (at(y, z, 1 - core), x, part)
    dev_head = (tm, x, 1 - part)
    dev_x = [None] + [(tm, lax.rem(x + k, SIDE), part) for k in (1, 2, 3)]

    barrier = pltpu.get_barrier_semaphore()
    friends = [dev_zup, dev_zdown, dev_yup, dev_ydown, dev_core, dev_head] + dev_x[1:]
    for friend in friends:
        pl.semaphore_signal(barrier, inc=1, device_id=friend, device_id_type=pl.DeviceIdType.MESH)

    def loads(h):
        columns = pl.ds(pl.multiple_of(h * HEAD_DIM, HEAD_DIM), HEAD_DIM)
        return (pltpu.make_async_copy(k_hbm.at[:, columns], kv.at[OWN, h, 0], load.at[h, 0]),
                pltpu.make_async_copy(v_hbm.at[:, columns], kv.at[OWN, h, 1], load.at[h, 1]))

    for h in range(heads):
        for copy in loads(h):
            copy.start()
    width = w_hbm.shape[2] // 2
    mine = pl.ds(pl.multiple_of(part * width, HEAD_DIM), width)
    load_w = pltpu.make_async_copy(w_hbm.at[:, :, mine], wbuf.at[:, pl.ds(0, HEAD_DIM), :], wload)
    load_w.start()

    has_yup = ym < SIDE - 1
    has_ydown = ym > 0
    edge1_out = (zm == 0) & has_yup
    edge1_in = (zm == 0) & has_ydown
    has_near = ((core == 0) & (chip > 0)) | ((core == 1) & (chip < SIDE * SIDE - 1))
    gives_near = ((core == 1) & (chip > 0)) | ((core == 0) & (chip < SIDE * SIDE - 1))
    near_at_edge = ((core == 1) & (z == 0)) | ((core == 0) & (z == SIDE - 1))
    near_slot = ZHI + core * (ZLO - ZHI)
    edge_slot = ZLO * (1 - far) + ZHI * far

    def remote(kind, h, src, dst, sem, device):
        return pltpu.make_async_remote_copy(
            src_ref=src, dst_ref=dst, send_sem=send.at[kind, h], recv_sem=sem,
            device_id=device, device_id_type=pl.DeviceIdType.MESH)

    def pair(kind, h, source, slot, device):
        return remote(kind, h, kv.at[source, h], kv.at[slot, h], recv.at[slot, h], device)

    def arrival(slot, h, device=None):
        return pair(TO_CORE, h, slot, slot, dev_core)

    def copies(kind, h):
        if kind == TO_ZUP:
            return pair(kind, h, OWN, ZLO, dev_zup)
        if kind == TO_ZDOWN:
            return pair(kind, h, OWN, ZHI, dev_zdown)
        if kind == RELAY_ZUP:
            return remote(kind, h, kv.at[ZLO, h, 0], kv.at[ZOP, h, 0], recv.at[ZOP, h], dev_zup)
        if kind == RELAY_ZDOWN:
            return remote(kind, h, kv.at[ZHI, h, 1], kv.at[ZOP, h, 1], recv_v.at[h], dev_zdown)
        if kind == TO_YDOWN:
            return pair(kind, h, OWN, YHI, dev_ydown)
        if kind == RELAY_YDOWN:
            return pair(kind, h, YHI, YOP, dev_ydown)
        if kind == TO_YUP:
            return pair(kind, h, OWN, YLO, dev_yup)
        if kind == TO_EDGE1:
            return pair(kind, h, edge_slot, EDGE1, dev_yup)
        if kind == TO_EDGE2:
            return pair(kind, h, ZOP, EDGE2, dev_yup)
        if kind == TO_XDOWN:
            return pair(kind, h, OWN, XHI, dev_x[3])
        if kind == TO_XUP:
            return pair(kind, h, OWN, XLO, dev_x[1])
        if kind == TO_CORE:
            return pair(kind, h, OWN, OTHER, dev_core)
        if kind == TO_HEAD:
            return remote(kind, h, att.at[h, :, pl.ds(0, HEAD_DIM)],
                          att.at[h, :, pl.ds(HEAD_DIM, HEAD_DIM)], att_recv.at[h], dev_head)

    def near_copy(h, source):
        return pair(TO_NEAR, h, source, NEAR, dev_core)

    def send_own(h):
        for copy in loads(h):
            copy.wait()
        for kind in (TO_ZUP, TO_ZDOWN, TO_YDOWN):
            copies(kind, h).start()

        @pl.when(has_yup)
        def _():
            copies(TO_YUP, h).start()

        @pl.when(x > 0)
        def _():
            copies(TO_XDOWN, h).start()

        @pl.when(x < SIDE - 1)
        def _():
            copies(TO_XUP, h).start()

        copies(TO_CORE, h).start()

    def relay(h):
        arrival(ZLO, h).wait_recv()
        copies(RELAY_ZUP, h).start()
        arrival(ZHI, h).wait_recv()
        copies(RELAY_ZDOWN, h).start()

        @pl.when(edge1_out)
        def _():
            copies(TO_EDGE1, h).start()

        @pl.when(gives_near & jnp.logical_not(near_at_edge))
        def _():
            near_copy(h, near_slot).start()

        arrival(YHI, h).wait_recv()
        copies(RELAY_YDOWN, h).start()

    def relay_again(h):
        copies(RELAY_ZUP, h).wait_recv()
        copies(RELAY_ZDOWN, h).wait_recv()

        @pl.when(has_yup)
        def _():
            copies(TO_EDGE2, h).start()

        @pl.when(edge1_in)
        def _():
            arrival(EDGE1, h).wait_recv()

        @pl.when(gives_near & near_at_edge)
        def _():
            near_copy(h, EDGE1).start()

    group = heads // 2
    chunk = width // SIDE

    def weight_piece(device, sem, column0):
        return pltpu.make_async_remote_copy(
            src_ref=w_hbm.at[pl.ds(core * group, group), :,
                             pl.ds(pl.multiple_of(column0 + x * chunk, HEAD_DIM), chunk)],
            dst_ref=wbuf.at[pl.ds(core * group, group), pl.ds(HEAD_DIM, HEAD_DIM),
                            pl.ds(pl.multiple_of(x * chunk, HEAD_DIM), chunk)],
            send_sem=wsend.at[sem], recv_sem=wrecv.at[sem],
            device_id=device, device_id_type=pl.DeviceIdType.MESH)

    def weight_relay(k):
        piece = wbuf.at[pl.ds(core * group, group), pl.ds(HEAD_DIM, HEAD_DIM),
                        pl.ds(pl.multiple_of(x * chunk, HEAD_DIM), chunk)]
        return pltpu.make_async_remote_copy(
            src_ref=piece, dst_ref=piece, send_sem=wsend.at[k], recv_sem=wrecv.at[k],
            device_id=dev_x[k], device_id_type=pl.DeviceIdType.MESH)

    def weight_cross():
        piece = wbuf.at[pl.ds(core * group, group), pl.ds(HEAD_DIM, HEAD_DIM), :]
        return pltpu.make_async_remote_copy(
            src_ref=piece, dst_ref=piece, send_sem=wsend.at[SIDE], recv_sem=wrecv.at[SIDE],
            device_id=dev_core, device_id_type=pl.DeviceIdType.MESH)

    frame = tm
    bands = SIDE
    valid = [1 + 0 * z, 1 + 0 * z, x > 0, x < SIDE - 1, has_ydown, has_yup, z < SIDE - 1, z > 0,
             1 + 0 * z, edge1_in, 1 + 0 * z, has_near, has_ydown]
    valid = [jnp.int32(v) if isinstance(v, int) else v.astype(jnp.int32) for v in valid]
    block_of = [
        frame * bands + x,
        (frame + 1 - 2 * core) * bands + x,
        frame * bands + x - 1,
        frame * bands + x + 1,
        (frame - 8 * sign) * bands + x,
        (frame + 8 * sign) * bands + x,
        (frame + 2) * bands + x,
        (frame - 2) * bands + x,
        at(y, lax.rem(z + 2, SIDE), core) * bands + x,
        (frame - 2 * sign) * bands + x,
        at(lax.rem(y + 2, SIDE), z, core) * bands + x,
        (frame - 1 + 2 * core) * bands + x,
        (frame - 4 * sign) * bands + x,
    ]

    def pick(values, i):
        return sum((i == k).astype(jnp.int32) * values[k] for k in range(SLOTS))

    def attend(slot, h, initial):
        if initial:
            shift = jnp.float32(0)
        else:
            block = pick(block_of, slot)
            hits = sum(((kv_list[0, j] == block) & (j < kv_count[0])).astype(jnp.int32)
                       for j in range(kv_list.shape[1]))
            shift = jnp.where(hits > 0, jnp.float32(0), jnp.float32(UNLISTED))
        columns = pl.ds(pl.multiple_of(h * HEAD_DIM, HEAD_DIM), HEAD_DIM)
        key_rows = kv[slot, h, 0]
        value_rows = kv[slot, h, 1]
        count = key_rows.shape[0] // HEAD_DIM
        for r in range(0, q_ref.shape[0], ROWS):
            rows = pl.ds(r, ROWS)
            scores = lax.dot_general(q_ref[rows, columns], key_rows, (((1,), (1,)), ((), ())),
                                     preferred_element_type=jnp.float32)
            parts = [scores[:, i * HEAD_DIM:(i + 1) * HEAD_DIM] for i in range(count)]
            highest = functools.reduce(jnp.maximum, parts)
            highest = jnp.max(highest, axis=1, keepdims=True) * SCORE_SCALE + shift
            highest = jnp.broadcast_to(highest, (ROWS, HEAD_DIM))
            if not initial:
                before = top[rows, :]
                highest = jnp.maximum(before, highest)
            base = highest - shift
            weights = [jnp.exp2(p * SCORE_SCALE - base) for p in parts]
            added = functools.reduce(jnp.add, weights)
            rounded = jnp.concatenate([w.astype(jnp.bfloat16) for w in weights], axis=1)
            update = jnp.dot(rounded, value_rows, preferred_element_type=jnp.float32)
            top[rows, :] = highest
            if initial:
                sums[rows, :] = added
                acc[rows, :] = update
            else:
                rescale = jnp.exp2(before - highest)
                sums[rows, :] = sums[rows, :] * rescale + added
                acc[rows, :] = acc[rows, :] * rescale + update

    def attend_all(h):
        attend(OWN, h, True)

        def one(slot, carry):
            @pl.when(pick(valid, slot) > 0)
            def _():
                @pl.when((slot <= YLO) | (slot >= YOP))
                def _():
                    arrival(slot, h).wait_recv()

                attend(slot, h, False)

            return carry

        lax.fori_loop(1, SLOTS, one, 0)
        att[h, :, pl.ds(0, HEAD_DIM)] = (
            acc[...] / jnp.sum(sums[...], axis=1, keepdims=True)).astype(jnp.bfloat16)

    step = HEAD_DIM * 4

    def project(h, last):
        for c in range(0, width, step):
            columns = pl.ds(c, step)
            term = jnp.dot(att[h], wbuf[h, :, columns], preferred_element_type=jnp.float32)
            if last:
                out_ref[:, columns] = (total[:, columns] + term).astype(jnp.bfloat16)
            else:
                total[:, columns] += term

    pl.semaphore_wait(barrier, len(friends))

    for h in range(AHEAD):
        send_own(h)
        if h == 0:
            weight_piece(dev_head, 0, (1 - part) * width).start()
    total[...] = jnp.zeros_like(total)
    load_w.wait()

    def turn(t, carry):
        @pl.when(t + AHEAD < heads)
        def _():
            send_own(t + AHEAD)

        @pl.when(t < heads)
        def _():
            relay(t)

        @pl.when(t == 0)
        def _():
            weight_piece(dev_head, 0, (1 - part) * width).wait_recv()
            for k in (1, 2, 3):
                weight_relay(k).start()

        @pl.when(t == 2)
        def _():
            weight_cross().wait_recv()

        @pl.when(t >= 2)
        def _():
            copies(TO_HEAD, t - 2).wait_recv()
            project(t - 2, False)

        @pl.when(t >= 1)
        def _():
            h = t - 1
            relay_again(h)
            attend_all(h)
            copies(TO_HEAD, h).start()

        @pl.when(t == 1)
        def _():
            for k in (1, 2, 3):
                weight_relay(k).wait_recv()
            weight_cross().start()

        return carry

    lax.fori_loop(0, heads + 1, turn, 0)
    copies(TO_HEAD, heads - 1).wait_recv()
    project(heads - 1, True)

    def drain(h, carry):
        for kind in (TO_ZUP, TO_ZDOWN, RELAY_ZUP, RELAY_ZDOWN, TO_YDOWN, RELAY_YDOWN,
                     TO_CORE, TO_HEAD):
            copies(kind, h).wait_send()

        @pl.when(has_yup)
        def _():
            copies(TO_YUP, h).wait_send()
            copies(TO_EDGE2, h).wait_send()

        @pl.when(edge1_out)
        def _():
            copies(TO_EDGE1, h).wait_send()

        @pl.when(x > 0)
        def _():
            copies(TO_XDOWN, h).wait_send()

        @pl.when(x < SIDE - 1)
        def _():
            copies(TO_XUP, h).wait_send()

        @pl.when(gives_near)
        def _():
            near_copy(h, OWN).wait_send()

        return carry

    lax.fori_loop(0, heads, drain, 0)
    weight_piece(dev_head, 0, (1 - part) * width).wait_send()
    for k in (1, 2, 3):
        weight_relay(k).wait_send()
    weight_cross().wait_send()


def body(queries, keys, values, out_weight, kv_list, kv_count):
    tokens, features = queries.shape
    heads = features // HEAD_DIM
    model = out_weight.shape[1]
    weight = out_weight.reshape(heads, HEAD_DIM, model)
    vmem = pl.BlockSpec(memory_space=pltpu.VMEM)
    smem = pl.BlockSpec(memory_space=pltpu.SMEM)
    anywhere = pl.BlockSpec(memory_space=pl.ANY)
    return pl.pallas_call(
        functools.partial(kernel, heads),
        out_shape=jax.ShapeDtypeStruct((tokens, model // 2), jnp.bfloat16),
        in_specs=[smem, smem, vmem, anywhere, anywhere, anywhere],
        out_specs=vmem,
        scratch_shapes=[
            pltpu.VMEM((SLOTS, heads, 2, tokens, HEAD_DIM), jnp.bfloat16),
            pltpu.VMEM((heads, tokens, 2 * HEAD_DIM), jnp.bfloat16),
            pltpu.VMEM((heads, 2 * HEAD_DIM, model // 2), jnp.bfloat16),
            pltpu.VMEM((tokens, model // 2), jnp.float32),
            pltpu.VMEM((tokens, HEAD_DIM), jnp.float32),
            pltpu.VMEM((tokens, HEAD_DIM), jnp.float32),
            pltpu.VMEM((tokens, HEAD_DIM), jnp.float32),
            pltpu.SemaphoreType.DMA((SENDS, heads)),
            pltpu.SemaphoreType.DMA((SLOTS, heads)),
            pltpu.SemaphoreType.DMA((heads,)),
            pltpu.SemaphoreType.DMA((heads,)),
            pltpu.SemaphoreType.DMA((heads, 2)),
            pltpu.SemaphoreType.DMA,
            pltpu.SemaphoreType.DMA((SIDE + 1,)),
            pltpu.SemaphoreType.DMA((SIDE + 1,)),
        ],
        compiler_params=pltpu.CompilerParams(
            collective_id=0, has_side_effects=True, vmem_limit_bytes=56 * 1024 * 1024),
    )(kv_list, kv_count, queries, keys, values, weight)


def solution(mesh):
    rows = P(("tm", "height"), "head")
    return jax.shard_map(
        body,
        mesh=mesh,
        in_specs=(rows, rows, rows, P("head", None), P(("tm", "height"), None),
                  P(("tm", "height"))),
        out_specs=rows,
        check_vma=False,
    )
```

```python
import functools

import jax
import jax.numpy as jnp
from jax import lax
from jax.experimental import pallas as pl
from jax.experimental.pallas import tpu as pltpu
from jax.sharding import PartitionSpec as P

HEAD_DIM = 128
SIDE = 4
SCORE_SCALE = HEAD_DIM ** (-0.5) * 1.4426950408889634
UNLISTED = -1e30
ROWS = 512
AHEAD = 1
EARLY = 2

OWN, OTHER, XLO, XHI, YLO, YHI, ZHI, ZLO, ZOP, EDGE1, YOP, NEAR, EDGE2 = range(13)
SLOTS = 13

(TO_ZUP, TO_ZDOWN, RELAY_ZUP, RELAY_ZDOWN, TO_YDOWN, RELAY_YDOWN, TO_YUP, TO_EDGE1,
 TO_EDGE2, TO_XDOWN, TO_XUP, TO_CORE, TO_NEAR, TO_HEAD) = range(14)
SENDS = 14


def kernel(heads, kv_list, kv_count, q_ref, k_hbm, v_hbm, w_hbm, out_ref,
           kv, att, wbuf, total, top, sums, acc,
           send, recv, recv_v, att_recv, load, wload, wsend, wrecv):
    tm = lax.axis_index("tm")
    x = lax.axis_index("height")
    part = lax.axis_index("head")
    core = lax.rem(tm, 2)
    chip = lax.div(tm, 2)
    z = lax.rem(chip, SIDE)
    y = lax.div(chip, SIDE)
    far = lax.div(z, 2)
    sign = 1 - 2 * far
    ym = y * (1 - far) + (SIDE - 1 - y) * far
    zm = z * (1 - far) + (SIDE - 1 - z) * far

    def at(yy, zz, cc):
        return (yy * SIDE + zz) * 2 + cc

    zup, zdown = lax.rem(z + 1, SIDE), lax.rem(z + 3, SIDE)
    yup, ydown = lax.rem(y + sign + SIDE, SIDE), lax.rem(y - sign + SIDE, SIDE)
    dev_zup = (at(y, zup, core), x, part)
    dev_zdown = (at(y, zdown, core), x, part)
    dev_yup = (at(yup, z, core), x, part)
    dev_ydown = (at(ydown, z, core), x, part)
    dev_core = (at(y, z, 1 - core), x, part)
    dev_head = (tm, x, 1 - part)
    dev_beside = (at(y, lax.rem(z + part + (1 - part) * 3, SIDE), core), x, 1 - part)
    dev_x = [None] + [(tm, lax.rem(x + k, SIDE), part) for k in (1, 2, 3)]

    barrier = pltpu.get_barrier_semaphore()
    friends = [dev_zup, dev_zdown, dev_yup, dev_ydown, dev_core, dev_head, dev_beside] + dev_x[1:]
    for friend in friends:
        pl.semaphore_signal(barrier, inc=1, device_id=friend, device_id_type=pl.DeviceIdType.MESH)

    def loads(h):
        columns = pl.ds(pl.multiple_of(h * HEAD_DIM, HEAD_DIM), HEAD_DIM)
        return (pltpu.make_async_copy(k_hbm.at[:, columns], kv.at[OWN, h, 0], load.at[h, 0]),
                pltpu.make_async_copy(v_hbm.at[:, columns], kv.at[OWN, h, 1], load.at[h, 1]))

    for h in range(heads):
        for copy in loads(h):
            copy.start()
    width = w_hbm.shape[2] // 2
    mine = pl.ds(pl.multiple_of(part * width, HEAD_DIM), width)
    load_w = pltpu.make_async_copy(w_hbm.at[:, :, mine], wbuf.at[:, pl.ds(0, HEAD_DIM), :], wload)
    load_w.start()

    has_yup = ym < SIDE - 1
    has_ydown = ym > 0
    edge1_out = (zm == 0) & has_yup
    edge1_in = (zm == 0) & has_ydown
    has_near = ((core == 0) & (chip > 0)) | ((core == 1) & (chip < SIDE * SIDE - 1))
    gives_near = ((core == 1) & (chip > 0)) | ((core == 0) & (chip < SIDE * SIDE - 1))
    near_at_edge = ((core == 1) & (z == 0)) | ((core == 0) & (z == SIDE - 1))
    near_slot = ZHI + core * (ZLO - ZHI)
    edge_slot = ZLO * (1 - far) + ZHI * far

    def remote(kind, h, src, dst, sem, device):
        return pltpu.make_async_remote_copy(
            src_ref=src, dst_ref=dst, send_sem=send.at[kind, h], recv_sem=sem,
            device_id=device, device_id_type=pl.DeviceIdType.MESH)

    def pair(kind, h, source, slot, device):
        return remote(kind, h, kv.at[source, h], kv.at[slot, h], recv.at[slot, h], device)

    def arrival(slot, h, device=None):
        return pair(TO_CORE, h, slot, slot, dev_core)

    def copies(kind, h):
        if kind == TO_ZUP:
            return pair(kind, h, OWN, ZLO, dev_zup)
        if kind == TO_ZDOWN:
            return pair(kind, h, OWN, ZHI, dev_zdown)
        if kind == RELAY_ZUP:
            return remote(kind, h, kv.at[ZLO, h, 0], kv.at[ZOP, h, 0], recv.at[ZOP, h], dev_zup)
        if kind == RELAY_ZDOWN:
            return remote(kind, h, kv.at[ZHI, h, 1], kv.at[ZOP, h, 1], recv_v.at[h], dev_zdown)
        if kind == TO_YDOWN:
            return pair(kind, h, OWN, YHI, dev_ydown)
        if kind == RELAY_YDOWN:
            return pair(kind, h, YHI, YOP, dev_ydown)
        if kind == TO_YUP:
            return pair(kind, h, OWN, YLO, dev_yup)
        if kind == TO_EDGE1:
            return pair(kind, h, edge_slot, EDGE1, dev_yup)
        if kind == TO_EDGE2:
            return pair(kind, h, ZOP, EDGE2, dev_yup)
        if kind == TO_XDOWN:
            return pair(kind, h, OWN, XHI, dev_x[3])
        if kind == TO_XUP:
            return pair(kind, h, OWN, XLO, dev_x[1])
        if kind == TO_CORE:
            return pair(kind, h, OWN, OTHER, dev_core)
        if kind == TO_HEAD:
            return remote(kind, h, att.at[h, :, pl.ds(0, HEAD_DIM)],
                          att.at[h, :, pl.ds(HEAD_DIM, HEAD_DIM)], att_recv.at[h], dev_head)

    def near_copy(h, source):
        return pair(TO_NEAR, h, source, NEAR, dev_core)

    def send_own(h):
        for copy in loads(h):
            copy.wait()
        for kind in (TO_ZUP, TO_ZDOWN, TO_YDOWN):
            copies(kind, h).start()

        @pl.when(has_yup)
        def _():
            copies(TO_YUP, h).start()

        @pl.when(x > 0)
        def _():
            copies(TO_XDOWN, h).start()

        @pl.when(x < SIDE - 1)
        def _():
            copies(TO_XUP, h).start()

        copies(TO_CORE, h).start()

    def relay(h):
        arrival(ZLO, h).wait_recv()
        copies(RELAY_ZUP, h).start()
        arrival(ZHI, h).wait_recv()
        copies(RELAY_ZDOWN, h).start()

        @pl.when(edge1_out)
        def _():
            copies(TO_EDGE1, h).start()

        @pl.when(gives_near & jnp.logical_not(near_at_edge))
        def _():
            near_copy(h, near_slot).start()

        arrival(YHI, h).wait_recv()
        copies(RELAY_YDOWN, h).start()

    def relay_again(h):
        copies(RELAY_ZUP, h).wait_recv()
        copies(RELAY_ZDOWN, h).wait_recv()

        @pl.when(has_yup)
        def _():
            copies(TO_EDGE2, h).start()

        @pl.when(edge1_in)
        def _():
            arrival(EDGE1, h).wait_recv()

        @pl.when(gives_near & near_at_edge)
        def _():
            near_copy(h, EDGE1).start()

    group = heads // 2
    chunk = width // SIDE

    def weight_piece(device, sem, column0):
        return pltpu.make_async_remote_copy(
            src_ref=w_hbm.at[pl.ds(core * group, group), :,
                             pl.ds(pl.multiple_of(column0 + x * chunk, HEAD_DIM), chunk)],
            dst_ref=wbuf.at[pl.ds(core * group, group), pl.ds(HEAD_DIM, HEAD_DIM),
                            pl.ds(pl.multiple_of(x * chunk, HEAD_DIM), chunk)],
            send_sem=wsend.at[sem], recv_sem=wrecv.at[sem],
            device_id=device, device_id_type=pl.DeviceIdType.MESH)

    def weight_relay(k):
        piece = wbuf.at[pl.ds(core * group, group), pl.ds(HEAD_DIM, HEAD_DIM),
                        pl.ds(pl.multiple_of(x * chunk, HEAD_DIM), chunk)]
        return pltpu.make_async_remote_copy(
            src_ref=piece, dst_ref=piece, send_sem=wsend.at[k], recv_sem=wrecv.at[k],
            device_id=dev_x[k], device_id_type=pl.DeviceIdType.MESH)

    def weight_cross():
        piece = wbuf.at[pl.ds(core * group, group), pl.ds(HEAD_DIM, HEAD_DIM), :]
        return pltpu.make_async_remote_copy(
            src_ref=piece, dst_ref=piece, send_sem=wsend.at[SIDE], recv_sem=wrecv.at[SIDE],
            device_id=dev_core, device_id_type=pl.DeviceIdType.MESH)

    frame = tm
    bands = SIDE
    valid = [1 + 0 * z, 1 + 0 * z, x > 0, x < SIDE - 1, has_ydown, has_yup, z < SIDE - 1, z > 0,
             1 + 0 * z, edge1_in, 1 + 0 * z, has_near, has_ydown]
    valid = [jnp.int32(v) if isinstance(v, int) else v.astype(jnp.int32) for v in valid]
    block_of = [
        frame * bands + x,
        (frame + 1 - 2 * core) * bands + x,
        frame * bands + x - 1,
        frame * bands + x + 1,
        (frame - 8 * sign) * bands + x,
        (frame + 8 * sign) * bands + x,
        (frame + 2) * bands + x,
        (frame - 2) * bands + x,
        at(y, lax.rem(z + 2, SIDE), core) * bands + x,
        (frame - 2 * sign) * bands + x,
        at(lax.rem(y + 2, SIDE), z, core) * bands + x,
        (frame - 1 + 2 * core) * bands + x,
        (frame - 4 * sign) * bands + x,
    ]

    def pick(values, i):
        return sum((i == k).astype(jnp.int32) * values[k] for k in range(SLOTS))

    def attend(slot, h, initial):
        if initial:
            shift = jnp.float32(0)
        else:
            block = pick(block_of, slot)
            hits = sum(((kv_list[0, j] == block) & (j < kv_count[0])).astype(jnp.int32)
                       for j in range(kv_list.shape[1]))
            shift = jnp.where(hits > 0, jnp.float32(0), jnp.float32(UNLISTED))
        columns = pl.ds(pl.multiple_of(h * HEAD_DIM, HEAD_DIM), HEAD_DIM)
        key_rows = kv[slot, h, 0]
        value_rows = kv[slot, h, 1]
        count = key_rows.shape[0] // HEAD_DIM
        for r in range(0, q_ref.shape[0], ROWS):
            rows = pl.ds(r, ROWS)
            scores = lax.dot_general(q_ref[rows, columns], key_rows, (((1,), (1,)), ((), ())),
                                     preferred_element_type=jnp.float32)
            parts = [scores[:, i * HEAD_DIM:(i + 1) * HEAD_DIM] for i in range(count)]
            highest = functools.reduce(jnp.maximum, parts)
            highest = jnp.max(highest, axis=1, keepdims=True) * SCORE_SCALE + shift
            highest = jnp.broadcast_to(highest, (ROWS, HEAD_DIM))
            if not initial:
                before = top[rows, :]
                highest = jnp.maximum(before, highest)
            base = highest - shift
            weights = [jnp.exp2(p * SCORE_SCALE - base) for p in parts]
            added = functools.reduce(jnp.add, weights)
            rounded = jnp.concatenate([w.astype(jnp.bfloat16) for w in weights], axis=1)
            update = jnp.dot(rounded, value_rows, preferred_element_type=jnp.float32)
            top[rows, :] = highest
            if initial:
                sums[rows, :] = added
                acc[rows, :] = update
            else:
                rescale = jnp.exp2(before - highest)
                sums[rows, :] = sums[rows, :] * rescale + added
                acc[rows, :] = acc[rows, :] * rescale + update

    def attend_all(h):
        attend(OWN, h, True)

        def one(slot, carry):
            @pl.when(pick(valid, slot) > 0)
            def _():
                @pl.when((slot <= YLO) | (slot >= YOP))
                def _():
                    arrival(slot, h).wait_recv()

                attend(slot, h, False)

            return carry

        lax.fori_loop(1, SLOTS, one, 0)
        att[h, :, pl.ds(0, HEAD_DIM)] = (
            acc[...] / jnp.sum(sums[...], axis=1, keepdims=True)).astype(jnp.bfloat16)

    step = HEAD_DIM * 4

    def project(h, last):
        for c in range(0, width, step):
            columns = pl.ds(c, step)
            term = jnp.dot(att[h], wbuf[h, :, columns], preferred_element_type=jnp.float32)
            if last:
                out_ref[:, columns] = (total[:, columns] + term).astype(jnp.bfloat16)
            else:
                total[:, columns] += term

    pl.semaphore_wait(barrier, len(friends))

    for h in range(AHEAD):
        send_own(h)
        if h == 0:
            weight_piece(dev_beside, 0, (1 - part) * width).start()
    total[...] = jnp.zeros_like(total)
    load_w.wait()

    def turn(t, carry):
        @pl.when(t + AHEAD < heads)
        def _():
            send_own(t + AHEAD)

        @pl.when(t < heads)
        def _():
            relay(t)

        @pl.when(t == heads - 1)
        def _():
            for early in range(EARLY):
                copies(TO_HEAD, early).start()

        @pl.when(t == 0)
        def _():
            weight_piece(dev_beside, 0, (1 - part) * width).wait_recv()
            for k in (1, 2, 3):
                weight_relay(k).start()

        @pl.when(t == 2)
        def _():
            weight_cross().wait_recv()

        @pl.when(t >= 1)
        def _():
            h = t - 1
            relay_again(h)

            @pl.when(t == heads)
            def _():
                for early in range(EARLY, heads - 1):
                    copies(TO_HEAD, early).start()

            attend_all(h)

        @pl.when(t == 1)
        def _():
            for k in (1, 2, 3):
                weight_relay(k).wait_recv()
            weight_cross().start()

        return carry

    lax.fori_loop(0, heads + 1, turn, 0)
    copies(TO_HEAD, heads - 1).start()

    def finish(h, carry):
        copies(TO_HEAD, h).wait_recv()
        project(h, False)
        return carry

    lax.fori_loop(0, heads - 1, finish, 0)
    copies(TO_HEAD, heads - 1).wait_recv()
    project(heads - 1, True)

    def drain(h, carry):
        for kind in (TO_ZUP, TO_ZDOWN, RELAY_ZUP, RELAY_ZDOWN, TO_YDOWN, RELAY_YDOWN,
                     TO_CORE, TO_HEAD):
            copies(kind, h).wait_send()

        @pl.when(has_yup)
        def _():
            copies(TO_YUP, h).wait_send()
            copies(TO_EDGE2, h).wait_send()

        @pl.when(edge1_out)
        def _():
            copies(TO_EDGE1, h).wait_send()

        @pl.when(x > 0)
        def _():
            copies(TO_XDOWN, h).wait_send()

        @pl.when(x < SIDE - 1)
        def _():
            copies(TO_XUP, h).wait_send()

        @pl.when(gives_near)
        def _():
            near_copy(h, OWN).wait_send()

        return carry

    lax.fori_loop(0, heads, drain, 0)
    weight_piece(dev_beside, 0, (1 - part) * width).wait_send()
    for k in (1, 2, 3):
        weight_relay(k).wait_send()
    weight_cross().wait_send()


def body(queries, keys, values, out_weight, kv_list, kv_count):
    tokens, features = queries.shape
    heads = features // HEAD_DIM
    model = out_weight.shape[1]
    weight = out_weight.reshape(heads, HEAD_DIM, model)
    vmem = pl.BlockSpec(memory_space=pltpu.VMEM)
    smem = pl.BlockSpec(memory_space=pltpu.SMEM)
    anywhere = pl.BlockSpec(memory_space=pl.ANY)
    return pl.pallas_call(
        functools.partial(kernel, heads),
        out_shape=jax.ShapeDtypeStruct((tokens, model // 2), jnp.bfloat16),
        in_specs=[smem, smem, vmem, anywhere, anywhere, anywhere],
        out_specs=vmem,
        scratch_shapes=[
            pltpu.VMEM((SLOTS, heads, 2, tokens, HEAD_DIM), jnp.bfloat16),
            pltpu.VMEM((heads, tokens, 2 * HEAD_DIM), jnp.bfloat16),
            pltpu.VMEM((heads, 2 * HEAD_DIM, model // 2), jnp.bfloat16),
            pltpu.VMEM((tokens, model // 2), jnp.float32),
            pltpu.VMEM((tokens, HEAD_DIM), jnp.float32),
            pltpu.VMEM((tokens, HEAD_DIM), jnp.float32),
            pltpu.VMEM((tokens, HEAD_DIM), jnp.float32),
            pltpu.SemaphoreType.DMA((SENDS, heads)),
            pltpu.SemaphoreType.DMA((SLOTS, heads)),
            pltpu.SemaphoreType.DMA((heads,)),
            pltpu.SemaphoreType.DMA((heads,)),
            pltpu.SemaphoreType.DMA((heads, 2)),
            pltpu.SemaphoreType.DMA,
            pltpu.SemaphoreType.DMA((SIDE + 1,)),
            pltpu.SemaphoreType.DMA((SIDE + 1,)),
        ],
        compiler_params=pltpu.CompilerParams(
            collective_id=0, has_side_effects=True, vmem_limit_bytes=56 * 1024 * 1024),
    )(kv_list, kv_count, queries, keys, values, weight)


def solution(mesh):
    rows = P(("tm", "height"), "head")
    return jax.shard_map(
        body,
        mesh=mesh,
        in_specs=(rows, rows, rows, P("head", None), P(("tm", "height"), None),
                  P(("tm", "height"))),
        out_specs=rows,
        check_vma=False,
    )
```

```python
import functools

import jax
import jax.numpy as jnp
from jax import lax
from jax.experimental import pallas as pl
from jax.experimental.pallas import tpu as pltpu
from jax.sharding import PartitionSpec as P

HEAD_DIM = 128
SIDE = 4
SCORE_SCALE = HEAD_DIM ** (-0.5) * 1.4426950408889634
UNLISTED = -1e30
ROWS = 512
AGAIN, ATTEND = 1, 2

OWN, OTHER, XLO, XHI, YHI, ZP, ZM, ZOP, YOP, YLO, EDGE1, NEAR, EDGE2 = range(13)
LATE = YLO
SLOTS = 13
SOURCE = 13

(TO_ZP, TO_ZM, RELAY_Z, TO_MATE, MATE_Q, TO_YDOWN, RELAY_YDOWN, LAST_YDOWN, TO_YUP, TO_EDGE1,
 TO_EDGE2, TO_XDOWN, TO_XUP, TO_CORE, TO_NEAR, TO_HEAD) = range(16)
SENDS = 16


def kernel(heads, kv_list, kv_count, q_hbm, k_hbm, v_hbm, w_hbm, out_ref,
           kv, queries, att, wbuf, total, top, sums, acc,
           send, recv, recv_v, q_recv, att_recv, load, wload, wsend, wrecv):
    tm = lax.axis_index("tm")
    x = lax.axis_index("height")
    part = lax.axis_index("head")
    core = lax.rem(tm, 2)
    chip = lax.div(tm, 2)
    z = lax.rem(chip, SIDE)
    y = lax.div(chip, SIDE)
    far = lax.div(z, 2)
    sign = 1 - 2 * far
    ym = y * (1 - far) + (SIDE - 1 - y) * far
    zm = z * (1 - far) + (SIDE - 1 - z) * far

    def at(yy, zz, cc):
        return (yy * SIDE + zz) * 2 + cc

    swapped = 1 - lax.rem(z, 2)
    half = part * (1 - swapped) + (1 - part) * swapped
    ahead = 1 - 2 * half
    z_ahead = lax.rem(z + ahead + SIDE, SIDE)
    z_back = lax.rem(z - ahead + SIDE, SIDE)
    z_out = z_ahead * swapped + z_back * (1 - swapped)
    yup, ydown = lax.rem(y + sign + SIDE, SIDE), lax.rem(y - sign + SIDE, SIDE)
    dev_zp = (at(y, z_out, core), x, part * swapped + (1 - part) * (1 - swapped))
    dev_zm = (at(y, z_ahead, core), x, 1 - part)
    dev_relay = (at(y, z_out, core), x, 1 - part)
    dev_back = (at(y, z_back, core), x, 1 - part)
    dev_far = (at(y, z_ahead, core), x, part)
    dev_yup = (at(yup, z, core), x, part)
    dev_ydown = (at(ydown, z, core), x, part)
    dev_core = (at(y, z, 1 - core), x, part)
    dev_head = (tm, x, 1 - part)
    dev_beside = (at(y, lax.rem(z + part + (1 - part) * 3, SIDE), core), x, 1 - part)
    dev_x = [None] + [(tm, lax.rem(x + k, SIDE), part) for k in (1, 2, 3)]

    barrier = pltpu.get_barrier_semaphore()
    friends = [dev_zm, dev_back, dev_far, dev_yup, dev_ydown, dev_core, dev_head] + dev_x[1:]
    for friend in friends:
        pl.semaphore_signal(barrier, inc=1, device_id=friend, device_id_type=pl.DeviceIdType.MESH)

    source = OWN + (SOURCE - OWN) * swapped

    def columns_of(h):
        return pl.ds(pl.multiple_of(h * HEAD_DIM, HEAD_DIM), HEAD_DIM)

    def loads(h):
        return (pltpu.make_async_copy(k_hbm.at[:, columns_of(h)], kv.at[source, h, 0], load.at[h, 0]),
                pltpu.make_async_copy(v_hbm.at[:, columns_of(h)], kv.at[source, h, 1], load.at[h, 1]))

    def load_q(h):
        return pltpu.make_async_copy(q_hbm.at[:, columns_of(h)], queries.at[h], load.at[h, 2])

    for h in range(heads):
        for copy in loads(h):
            copy.start()

        @pl.when(swapped == 0)
        def _():
            load_q(h).start()

    width = w_hbm.shape[2] // 2

    def rows_of(heads_half):
        return pl.ds(pl.multiple_of(heads_half * HEAD_DIM, HEAD_DIM), HEAD_DIM)

    mine = pl.ds(pl.multiple_of(part * width, HEAD_DIM), width)
    load_w = pltpu.make_async_copy(w_hbm.at[:, :, mine], wbuf.at[:, rows_of(part), :], wload)
    load_w.start()

    has_yup = ym < SIDE - 1
    has_ydown = ym > 0
    edge1_out = (zm == 0) & has_yup
    edge1_in = (zm == 0) & has_ydown
    has_near = ((core == 0) & (chip > 0)) | ((core == 1) & (chip < SIDE * SIDE - 1))
    gives_near = ((core == 1) & (chip > 0)) | ((core == 0) & (chip < SIDE * SIDE - 1))
    near_at_edge = ((core == 1) & (z == 0)) | ((core == 0) & (z == SIDE - 1))
    half_is_first = 1 - half
    slot_after = ZM + (ZP - ZM) * half_is_first
    slot_before = ZP + (ZM - ZP) * half_is_first
    near_slot = slot_after * (1 - core) + slot_before * core
    edge_slot = slot_before * (1 - far) + slot_after * far
    relay_slot = ZP + (ZM - ZP) * swapped
    late_slot = ZM + (ZP - ZM) * swapped

    def remote(kind, h, src, dst, sem, device):
        return pltpu.make_async_remote_copy(
            src_ref=src, dst_ref=dst, send_sem=send.at[kind, h], recv_sem=sem,
            device_id=device, device_id_type=pl.DeviceIdType.MESH)

    def pair(kind, h, source, slot, device):
        return remote(kind, h, kv.at[source, h], kv.at[slot, h], recv.at[slot, h], device)

    def arrival(slot, h, device=None):
        return pair(TO_CORE, h, slot, slot, dev_core)

    def copies(kind, h):
        if kind == TO_ZP:
            return pair(kind, h, source, ZP, dev_zp)
        if kind == TO_ZM:
            return pair(kind, h, OWN, ZM, dev_zm)
        if kind == RELAY_Z:
            return pair(kind, h, relay_slot, ZOP, dev_relay)
        if kind == TO_MATE:
            return pair(kind, h, SOURCE, OWN, dev_head)
        if kind == MATE_Q:
            return remote(kind, h, q_hbm.at[:, columns_of(h)], queries.at[h], q_recv.at[h], dev_head)
        if kind == TO_YDOWN:
            return pair(kind, h, OWN, YHI, dev_ydown)
        if kind == RELAY_YDOWN:
            return pair(kind, h, YHI, YOP, dev_ydown)
        if kind == TO_YUP:
            return remote(kind, h, kv.at[OWN, h, 0], kv.at[YLO, h, 0], recv.at[YLO, h], dev_yup)
        if kind == LAST_YDOWN:
            return remote(kind, h, kv.at[YOP, h, 1], kv.at[YLO, h, 1], recv_v.at[h], dev_ydown)
        if kind == TO_EDGE1:
            return pair(kind, h, edge_slot, EDGE1, dev_yup)
        if kind == TO_EDGE2:
            return pair(kind, h, ZOP, EDGE2, dev_yup)
        if kind == TO_XDOWN:
            return pair(kind, h, OWN, XHI, dev_x[3])
        if kind == TO_XUP:
            return pair(kind, h, OWN, XLO, dev_x[1])
        if kind == TO_CORE:
            return pair(kind, h, OWN, OTHER, dev_core)
        if kind == TO_HEAD:
            piece = att.at[h, :, rows_of(half)]
            return remote(kind, h, piece, piece, att_recv.at[h], dev_head)

    def near_copy(h, slot):
        return pair(TO_NEAR, h, slot, NEAR, dev_core)

    def give(h):
        for copy in loads(h):
            copy.wait()

        @pl.when(swapped == 1)
        def _():
            copies(TO_MATE, h).start()

    def send_own(h):
        copies(TO_ZP, h).start()

        @pl.when(swapped == 1)
        def _():
            arrival(OWN, h).wait_recv()
            copies(MATE_Q, h).start()

        for kind in (TO_ZM, TO_YDOWN):
            copies(kind, h).start()

        @pl.when(has_yup)
        def _():
            copies(TO_YUP, h).start()

        @pl.when(x > 0)
        def _():
            copies(TO_XDOWN, h).start()

        @pl.when(x < SIDE - 1)
        def _():
            copies(TO_XUP, h).start()

        copies(TO_CORE, h).start()

    def relay(h):
        arrival(relay_slot, h).wait_recv()
        copies(RELAY_Z, h).start()
        arrival(YHI, h).wait_recv()
        copies(RELAY_YDOWN, h).start()

    def relay_again(h):
        arrival(late_slot, h).wait_recv()

        @pl.when(edge1_out)
        def _():
            copies(TO_EDGE1, h).start()

        @pl.when(gives_near & jnp.logical_not(near_at_edge))
        def _():
            near_copy(h, near_slot).start()

        arrival(YOP, h).wait_recv()

        @pl.when(ym != 1)
        def _():
            copies(LAST_YDOWN, h).start()

        arrival(ZOP, h).wait_recv()

        @pl.when(has_yup)
        def _():
            copies(TO_EDGE2, h).start()

    def relay_edge(h):
        @pl.when(has_ydown)
        def _():
            copies(TO_YUP, h).wait_recv()
            copies(LAST_YDOWN, h).wait_recv()

        @pl.when(edge1_in)
        def _():
            arrival(EDGE1, h).wait_recv()

        @pl.when(gives_near & near_at_edge)
        def _():
            near_copy(h, EDGE1).start()

    group = heads // 2
    chunk = width // SIDE

    def weight_piece():
        return pltpu.make_async_remote_copy(
            src_ref=w_hbm.at[pl.ds(core * group, group), :,
                             pl.ds(pl.multiple_of((1 - part) * width + x * chunk, HEAD_DIM), chunk)],
            dst_ref=wbuf.at[pl.ds(core * group, group), rows_of(part),
                            pl.ds(pl.multiple_of(x * chunk, HEAD_DIM), chunk)],
            send_sem=wsend.at[0], recv_sem=wrecv.at[0],
            device_id=dev_beside, device_id_type=pl.DeviceIdType.MESH)

    def weight_relay(k):
        piece = wbuf.at[pl.ds(core * group, group), rows_of(1 - part),
                        pl.ds(pl.multiple_of(x * chunk, HEAD_DIM), chunk)]
        return pltpu.make_async_remote_copy(
            src_ref=piece, dst_ref=piece, send_sem=wsend.at[k], recv_sem=wrecv.at[k],
            device_id=dev_x[k], device_id_type=pl.DeviceIdType.MESH)

    def weight_cross():
        piece = wbuf.at[pl.ds(core * group, group), rows_of(1 - part), :]
        return pltpu.make_async_remote_copy(
            src_ref=piece, dst_ref=piece, send_sem=wsend.at[SIDE], recv_sem=wrecv.at[SIDE],
            device_id=dev_core, device_id_type=pl.DeviceIdType.MESH)

    frame = tm
    bands = SIDE
    always = 1 + 0 * z
    valid = [always, always, x > 0, x < SIDE - 1, has_yup, (z + ahead >= 0) & (z + ahead < SIDE),
             (z - ahead >= 0) & (z - ahead < SIDE), always, always, has_ydown, edge1_in, has_near,
             has_ydown]
    valid = [jnp.int32(v) if isinstance(v, int) else v.astype(jnp.int32) for v in valid]
    block_of = [
        frame * bands + x,
        (frame + 1 - 2 * core) * bands + x,
        frame * bands + x - 1,
        frame * bands + x + 1,
        (frame + 8 * sign) * bands + x,
        (frame + 2 * ahead) * bands + x,
        (frame - 2 * ahead) * bands + x,
        at(y, lax.rem(z + 2, SIDE), core) * bands + x,
        at(lax.rem(y + 2, SIDE), z, core) * bands + x,
        (frame - 8 * sign) * bands + x,
        (frame - 2 * sign) * bands + x,
        (frame - 1 + 2 * core) * bands + x,
        (frame - 4 * sign) * bands + x,
    ]

    def pick(values, i):
        return sum((i == k).astype(jnp.int32) * values[k] for k in range(SLOTS))

    def attend(slot, h, initial):
        if initial:
            shift = jnp.float32(0)
        else:
            block = pick(block_of, slot)
            hits = sum(((kv_list[0, j] == block) & (j < kv_count[0])).astype(jnp.int32)
                       for j in range(kv_list.shape[1]))
            shift = jnp.where(hits > 0, jnp.float32(0), jnp.float32(UNLISTED))
        here = lax.rem(h, 2)
        key_rows = kv[slot, h, 0]
        value_rows = kv[slot, h, 1]
        count = key_rows.shape[0] // HEAD_DIM
        for r in range(0, queries.shape[1], ROWS):
            rows = pl.ds(r, ROWS)
            scores = lax.dot_general(queries[h, rows, :], key_rows, (((1,), (1,)), ((), ())),
                                     preferred_element_type=jnp.float32)
            parts = [scores[:, i * HEAD_DIM:(i + 1) * HEAD_DIM] for i in range(count)]
            highest = functools.reduce(jnp.maximum, parts)
            highest = jnp.max(highest, axis=1, keepdims=True) * SCORE_SCALE + shift
            highest = jnp.broadcast_to(highest, (ROWS, HEAD_DIM))
            if not initial:
                before = top[here, rows, :]
                highest = jnp.maximum(before, highest)
            base = highest - shift
            weights = [jnp.exp2(p * SCORE_SCALE - base) for p in parts]
            added = functools.reduce(jnp.add, weights)
            rounded = jnp.concatenate([w.astype(jnp.bfloat16) for w in weights], axis=1)
            update = jnp.dot(rounded, value_rows, preferred_element_type=jnp.float32)
            top[here, rows, :] = highest
            if initial:
                sums[here, rows, :] = added
                acc[here, rows, :] = update
            else:
                rescale = jnp.exp2(before - highest)
                sums[here, rows, :] = sums[here, rows, :] * rescale + added
                acc[here, rows, :] = acc[here, rows, :] * rescale + update

    def attend_slots(h, first, last):
        def one(slot, carry):
            @pl.when(pick(valid, slot) > 0)
            def _():
                @pl.when((slot <= XHI) | (slot >= NEAR))
                def _():
                    arrival(slot, h).wait_recv()

                attend(slot, h, False)

            return carry

        lax.fori_loop(first, last, one, 0)

    def attend_early(h):
        @pl.when(swapped == 1)
        def _():
            copies(MATE_Q, h).wait_recv()

        @pl.when(swapped == 0)
        def _():
            load_q(h).wait()

        attend(OWN, h, True)
        attend_slots(h, OTHER, LATE)

    def attend_late(h):
        attend_slots(h, LATE, SLOTS)
        here = lax.rem(h, 2)
        att[h, :, rows_of(half)] = (
            acc[here] / jnp.sum(sums[here], axis=1, keepdims=True)).astype(jnp.bfloat16)

    step = HEAD_DIM * 4

    def project(h, last):
        for c in range(0, width, step):
            columns = pl.ds(c, step)
            term = jnp.dot(att[h], wbuf[h, :, columns], preferred_element_type=jnp.float32)
            if last:
                out_ref[:, columns] = (total[:, columns] + term).astype(jnp.bfloat16)
            else:
                total[:, columns] += term

    pl.semaphore_wait(barrier, len(friends))

    give(0)
    send_own(0)
    give(1)
    total[...] = jnp.zeros_like(total)

    def turn(t, carry):
        @pl.when((t >= AGAIN) & (t < heads + AGAIN))
        def _():
            relay_again(t - AGAIN)

        @pl.when(t < heads)
        def _():
            relay(t)

        @pl.when(t + 1 < heads)
        def _():
            send_own(t + 1)

        @pl.when(t + 2 < heads)
        def _():
            give(t + 2)

        @pl.when(t == 1)
        def _():
            weight_piece().start()

        @pl.when(t == 3)
        def _():
            weight_piece().wait_recv()
            for k in (1, 2, 3):
                weight_relay(k).start()

        @pl.when(t == 5)
        def _():
            for k in (1, 2, 3):
                weight_relay(k).wait_recv()
            weight_cross().start()

        @pl.when(t >= ATTEND)
        def _():
            relay_edge(t - ATTEND)
            attend_late(t - ATTEND)
            copies(TO_HEAD, t - ATTEND).start()

        @pl.when((t >= 1) & (t <= heads))
        def _():
            attend_early(t - 1)

        return carry

    lax.fori_loop(0, heads + ATTEND, turn, 0)
    load_w.wait()
    weight_cross().wait_recv()

    def finish(h, carry):
        copies(TO_HEAD, h).wait_recv()
        project(h, False)
        return carry

    lax.fori_loop(0, heads - 1, finish, 0)
    copies(TO_HEAD, heads - 1).wait_recv()
    project(heads - 1, True)

    def drain(h, carry):
        for kind in (TO_ZP, TO_ZM, RELAY_Z, TO_YDOWN, RELAY_YDOWN, TO_CORE, TO_HEAD):
            copies(kind, h).wait_send()

        @pl.when(swapped == 1)
        def _():
            copies(TO_MATE, h).wait_send()
            copies(MATE_Q, h).wait_send()

        @pl.when(ym != 1)
        def _():
            copies(LAST_YDOWN, h).wait_send()

        @pl.when(has_yup)
        def _():
            copies(TO_YUP, h).wait_send()
            copies(TO_EDGE2, h).wait_send()

        @pl.when(edge1_out)
        def _():
            copies(TO_EDGE1, h).wait_send()

        @pl.when(x > 0)
        def _():
            copies(TO_XDOWN, h).wait_send()

        @pl.when(x < SIDE - 1)
        def _():
            copies(TO_XUP, h).wait_send()

        @pl.when(gives_near)
        def _():
            near_copy(h, OWN).wait_send()

        return carry

    lax.fori_loop(0, heads, drain, 0)
    weight_piece().wait_send()
    for k in (1, 2, 3):
        weight_relay(k).wait_send()
    weight_cross().wait_send()


def body(queries, keys, values, out_weight, kv_list, kv_count):
    tokens, features = queries.shape
    heads = features // HEAD_DIM
    model = out_weight.shape[1]
    weight = out_weight.reshape(heads, HEAD_DIM, model)
    vmem = pl.BlockSpec(memory_space=pltpu.VMEM)
    smem = pl.BlockSpec(memory_space=pltpu.SMEM)
    anywhere = pl.BlockSpec(memory_space=pl.ANY)
    return pl.pallas_call(
        functools.partial(kernel, heads),
        out_shape=jax.ShapeDtypeStruct((tokens, model // 2), jnp.bfloat16),
        in_specs=[smem, smem, anywhere, anywhere, anywhere, anywhere],
        out_specs=vmem,
        scratch_shapes=[
            pltpu.VMEM((SLOTS + 1, heads, 2, tokens, HEAD_DIM), jnp.bfloat16),
            pltpu.VMEM((heads, tokens, HEAD_DIM), jnp.bfloat16),
            pltpu.VMEM((heads, tokens, 2 * HEAD_DIM), jnp.bfloat16),
            pltpu.VMEM((heads, 2 * HEAD_DIM, model // 2), jnp.bfloat16),
            pltpu.VMEM((tokens, model // 2), jnp.float32),
            pltpu.VMEM((2, tokens, HEAD_DIM), jnp.float32),
            pltpu.VMEM((2, tokens, HEAD_DIM), jnp.float32),
            pltpu.VMEM((2, tokens, HEAD_DIM), jnp.float32),
            pltpu.SemaphoreType.DMA((SENDS, heads)),
            pltpu.SemaphoreType.DMA((SLOTS, heads)),
            pltpu.SemaphoreType.DMA((heads,)),
            pltpu.SemaphoreType.DMA((heads,)),
            pltpu.SemaphoreType.DMA((heads,)),
            pltpu.SemaphoreType.DMA((heads, 3)),
            pltpu.SemaphoreType.DMA,
            pltpu.SemaphoreType.DMA((SIDE + 1,)),
            pltpu.SemaphoreType.DMA((SIDE + 1,)),
        ],
        compiler_params=pltpu.CompilerParams(
            collective_id=0, has_side_effects=True, vmem_limit_bytes=56 * 1024 * 1024),
    )(kv_list, kv_count, queries, keys, values, weight)


def solution(mesh):
    rows = P(("tm", "height"), "head")
    return jax.shard_map(
        body,
        mesh=mesh,
        in_specs=(rows, rows, rows, P("head", None), P(("tm", "height"), None),
                  P(("tm", "height"))),
        out_specs=rows,
        check_vma=False,
    )
```

```python
import functools

import jax
import jax.numpy as jnp
from jax import lax
from jax.experimental import pallas as pl
from jax.experimental.pallas import tpu as pltpu
from jax.sharding import PartitionSpec as P

HEAD_DIM = 128
SIDE = 4
SCORE_SCALE = HEAD_DIM ** (-0.5) * 1.4426950408889634
UNLISTED = -1e30
ROWS = 512
AGAIN, ATTEND = 1, 2

OWN, OTHER, XLO, XHI, YHI, ZP, ZM, ZOP, YOP, YLO, EDGE1, NEAR, EDGE2 = range(13)
LATE = YLO
SLOTS = 13
SOURCE = 13

(TO_ZP, TO_ZM, RELAY_Z, TO_MATE, MATE_Q, TO_YDOWN, RELAY_YDOWN, LAST_YDOWN, TO_YUP, TO_EDGE1,
 TO_EDGE2, TO_XDOWN, TO_XUP, TO_CORE, TO_NEAR, TO_HEAD) = range(16)
SENDS = 16


def kernel(heads, kv_list, kv_count, q_hbm, k_hbm, v_hbm, w_hbm, out_ref,
           kv, queries, att, wbuf, total, top, sums, acc,
           send, recv, recv_v, q_recv, att_recv, load, wload, wsend, wrecv):
    tm = lax.axis_index("tm")
    x = lax.axis_index("height")
    part = lax.axis_index("head")
    core = lax.rem(tm, 2)
    chip = lax.div(tm, 2)
    z = lax.rem(chip, SIDE)
    y = lax.div(chip, SIDE)
    far = lax.div(z, 2)
    sign = 1 - 2 * far
    ym = y * (1 - far) + (SIDE - 1 - y) * far
    zm = z * (1 - far) + (SIDE - 1 - z) * far

    def at(yy, zz, cc):
        return (yy * SIDE + zz) * 2 + cc

    swapped = 1 - lax.rem(z, 2)
    half = part * (1 - swapped) + (1 - part) * swapped
    ahead = 1 - 2 * half
    z_ahead = lax.rem(z + ahead + SIDE, SIDE)
    z_back = lax.rem(z - ahead + SIDE, SIDE)
    z_out = z_ahead * swapped + z_back * (1 - swapped)
    yup, ydown = lax.rem(y + sign + SIDE, SIDE), lax.rem(y - sign + SIDE, SIDE)
    dev_zp = (at(y, z_out, core), x, part * swapped + (1 - part) * (1 - swapped))
    dev_zm = (at(y, z_ahead, core), x, 1 - part)
    dev_relay = (at(y, z_out, core), x, 1 - part)
    dev_back = (at(y, z_back, core), x, 1 - part)
    dev_far = (at(y, z_ahead, core), x, part)
    dev_yup = (at(yup, z, core), x, part)
    dev_ydown = (at(ydown, z, core), x, part)
    dev_core = (at(y, z, 1 - core), x, part)
    dev_head = (tm, x, 1 - part)
    dev_beside = (at(y, lax.rem(z + part + (1 - part) * 3, SIDE), core), x, 1 - part)
    dev_x = [None] + [(tm, lax.rem(x + k, SIDE), part) for k in (1, 2, 3)]

    barrier = pltpu.get_barrier_semaphore()
    friends = [dev_zm, dev_back, dev_far, dev_yup, dev_ydown, dev_core, dev_head] + dev_x[1:]
    for friend in friends:
        pl.semaphore_signal(barrier, inc=1, device_id=friend, device_id_type=pl.DeviceIdType.MESH)

    source = OWN + (SOURCE - OWN) * swapped

    def columns_of(h):
        return pl.ds(pl.multiple_of(h * HEAD_DIM, HEAD_DIM), HEAD_DIM)

    def loads(h):
        return (pltpu.make_async_copy(k_hbm.at[:, columns_of(h)], kv.at[source, h, 0], load.at[h, 0]),
                pltpu.make_async_copy(v_hbm.at[:, columns_of(h)], kv.at[source, h, 1], load.at[h, 1]))

    def load_q(h):
        return pltpu.make_async_copy(q_hbm.at[:, columns_of(h)], queries.at[h], load.at[h, 2])

    for h in range(heads):
        for copy in loads(h):
            copy.start()

        @pl.when(swapped == 0)
        def _():
            load_q(h).start()

    width = w_hbm.shape[2] // 2

    def rows_of(heads_half):
        return pl.ds(pl.multiple_of(heads_half * HEAD_DIM, HEAD_DIM), HEAD_DIM)

    mine = pl.ds(pl.multiple_of(part * width, HEAD_DIM), width)
    load_w = pltpu.make_async_copy(w_hbm.at[:, :, mine], wbuf.at[:, rows_of(part), :], wload)
    load_w.start()

    has_yup = ym < SIDE - 1
    has_ydown = ym > 0
    edge1_out = (zm == 0) & has_yup
    edge1_in = (zm == 0) & has_ydown
    has_near = ((core == 0) & (chip > 0)) | ((core == 1) & (chip < SIDE * SIDE - 1))
    gives_near = ((core == 1) & (chip > 0)) | ((core == 0) & (chip < SIDE * SIDE - 1))
    near_at_edge = ((core == 1) & (z == 0)) | ((core == 0) & (z == SIDE - 1))
    half_is_first = 1 - half
    slot_after = ZM + (ZP - ZM) * half_is_first
    slot_before = ZP + (ZM - ZP) * half_is_first
    near_slot = slot_after * (1 - core) + slot_before * core
    edge_slot = slot_before * (1 - far) + slot_after * far
    relay_slot = ZP + (ZM - ZP) * swapped
    late_slot = ZM + (ZP - ZM) * swapped

    def remote(kind, h, src, dst, sem, device):
        return pltpu.make_async_remote_copy(
            src_ref=src, dst_ref=dst, send_sem=send.at[kind, h], recv_sem=sem,
            device_id=device, device_id_type=pl.DeviceIdType.MESH)

    def pair(kind, h, source, slot, device):
        return remote(kind, h, kv.at[source, h], kv.at[slot, h], recv.at[slot, h], device)

    def arrival(slot, h, device=None):
        return pair(TO_CORE, h, slot, slot, dev_core)

    def copies(kind, h):
        if kind == TO_ZP:
            return pair(kind, h, source, ZP, dev_zp)
        if kind == TO_ZM:
            return pair(kind, h, OWN, ZM, dev_zm)
        if kind == RELAY_Z:
            return pair(kind, h, relay_slot, ZOP, dev_relay)
        if kind == TO_MATE:
            return pair(kind, h, SOURCE, OWN, dev_head)
        if kind == MATE_Q:
            return remote(kind, h, q_hbm.at[:, columns_of(h)], queries.at[h], q_recv.at[h], dev_head)
        if kind == TO_YDOWN:
            return pair(kind, h, OWN, YHI, dev_ydown)
        if kind == RELAY_YDOWN:
            return pair(kind, h, YHI, YOP, dev_ydown)
        if kind == TO_YUP:
            return remote(kind, h, kv.at[OWN, h, 0], kv.at[YLO, h, 0], recv.at[YLO, h], dev_yup)
        if kind == LAST_YDOWN:
            return remote(kind, h, kv.at[YOP, h, 1], kv.at[YLO, h, 1], recv_v.at[h], dev_ydown)
        if kind == TO_EDGE1:
            return pair(kind, h, edge_slot, EDGE1, dev_yup)
        if kind == TO_EDGE2:
            return pair(kind, h, ZOP, EDGE2, dev_yup)
        if kind == TO_XDOWN:
            return pair(kind, h, OWN, XHI, dev_x[3])
        if kind == TO_XUP:
            return pair(kind, h, OWN, XLO, dev_x[1])
        if kind == TO_CORE:
            return pair(kind, h, OWN, OTHER, dev_core)
        if kind == TO_HEAD:
            piece = att.at[h, :, rows_of(half)]
            return remote(kind, h, piece, piece, att_recv.at[h], dev_head)

    def near_copy(h, slot):
        return pair(TO_NEAR, h, slot, NEAR, dev_core)

    def give(h):
        for copy in loads(h):
            copy.wait()

        @pl.when(swapped == 1)
        def _():
            copies(TO_MATE, h).start()

    def send_own(h):
        copies(TO_ZP, h).start()

        @pl.when(swapped == 1)
        def _():
            arrival(OWN, h).wait_recv()
            copies(MATE_Q, h).start()

        for kind in (TO_ZM, TO_YDOWN):
            copies(kind, h).start()

        @pl.when(has_yup)
        def _():
            copies(TO_YUP, h).start()

        @pl.when(x > 0)
        def _():
            copies(TO_XDOWN, h).start()

        @pl.when(x < SIDE - 1)
        def _():
            copies(TO_XUP, h).start()

        copies(TO_CORE, h).start()

    def relay(h):
        arrival(relay_slot, h).wait_recv()
        copies(RELAY_Z, h).start()
        arrival(YHI, h).wait_recv()
        copies(RELAY_YDOWN, h).start()

    def relay_again(h):
        arrival(late_slot, h).wait_recv()

        @pl.when(edge1_out)
        def _():
            copies(TO_EDGE1, h).start()

        @pl.when(gives_near & jnp.logical_not(near_at_edge))
        def _():
            near_copy(h, near_slot).start()

        arrival(YOP, h).wait_recv()

        @pl.when(ym != 1)
        def _():
            copies(LAST_YDOWN, h).start()

        arrival(ZOP, h).wait_recv()

        @pl.when(has_yup)
        def _():
            copies(TO_EDGE2, h).start()

    def relay_edge(h):
        @pl.when(has_ydown)
        def _():
            copies(TO_YUP, h).wait_recv()
            copies(LAST_YDOWN, h).wait_recv()

        @pl.when(edge1_in)
        def _():
            arrival(EDGE1, h).wait_recv()

        @pl.when(gives_near & near_at_edge)
        def _():
            near_copy(h, EDGE1).start()

    group = heads // 2
    chunk = width // SIDE

    def weight_piece(sem=0, device=dev_beside):
        return pltpu.make_async_remote_copy(
            src_ref=w_hbm.at[pl.ds(core * group, group), :,
                             pl.ds(pl.multiple_of((1 - part) * width + x * chunk, HEAD_DIM), chunk)],
            dst_ref=wbuf.at[pl.ds(core * group, group), rows_of(part),
                            pl.ds(pl.multiple_of(x * chunk, HEAD_DIM), chunk)],
            send_sem=wsend.at[sem], recv_sem=wrecv.at[0],
            device_id=device, device_id_type=pl.DeviceIdType.MESH)

    def weight_relay(k):
        piece = wbuf.at[pl.ds(core * group, group), rows_of(1 - part),
                        pl.ds(pl.multiple_of(x * chunk, HEAD_DIM), chunk)]
        return pltpu.make_async_remote_copy(
            src_ref=piece, dst_ref=piece, send_sem=wsend.at[k], recv_sem=wrecv.at[k],
            device_id=dev_x[k], device_id_type=pl.DeviceIdType.MESH)

    def weight_cross():
        piece = wbuf.at[pl.ds(core * group, group), rows_of(1 - part), :]
        return pltpu.make_async_remote_copy(
            src_ref=piece, dst_ref=piece, send_sem=wsend.at[SIDE], recv_sem=wrecv.at[SIDE],
            device_id=dev_core, device_id_type=pl.DeviceIdType.MESH)

    frame = tm
    bands = SIDE
    always = 1 + 0 * z
    valid = [always, always, x > 0, x < SIDE - 1, has_yup, (z + ahead >= 0) & (z + ahead < SIDE),
             (z - ahead >= 0) & (z - ahead < SIDE), always, always, has_ydown, edge1_in, has_near,
             has_ydown]
    valid = [jnp.int32(v) if isinstance(v, int) else v.astype(jnp.int32) for v in valid]
    block_of = [
        frame * bands + x,
        (frame + 1 - 2 * core) * bands + x,
        frame * bands + x - 1,
        frame * bands + x + 1,
        (frame + 8 * sign) * bands + x,
        (frame + 2 * ahead) * bands + x,
        (frame - 2 * ahead) * bands + x,
        at(y, lax.rem(z + 2, SIDE), core) * bands + x,
        at(lax.rem(y + 2, SIDE), z, core) * bands + x,
        (frame - 8 * sign) * bands + x,
        (frame - 2 * sign) * bands + x,
        (frame - 1 + 2 * core) * bands + x,
        (frame - 4 * sign) * bands + x,
    ]

    def pick(values, i):
        return sum((i == k).astype(jnp.int32) * values[k] for k in range(SLOTS))

    def attend(slot, h, initial):
        if initial:
            shift = jnp.float32(0)
        else:
            block = pick(block_of, slot)
            hits = sum(((kv_list[0, j] == block) & (j < kv_count[0])).astype(jnp.int32)
                       for j in range(kv_list.shape[1]))
            shift = jnp.where(hits > 0, jnp.float32(0), jnp.float32(UNLISTED))
        here = lax.rem(h, 2)
        key_rows = kv[slot, h, 0]
        value_rows = kv[slot, h, 1]
        count = key_rows.shape[0] // HEAD_DIM
        for r in range(0, queries.shape[1], ROWS):
            rows = pl.ds(r, ROWS)
            scores = lax.dot_general(queries[h, rows, :], key_rows, (((1,), (1,)), ((), ())),
                                     preferred_element_type=jnp.float32)
            parts = [scores[:, i * HEAD_DIM:(i + 1) * HEAD_DIM] for i in range(count)]
            highest = functools.reduce(jnp.maximum, parts)
            highest = jnp.max(highest, axis=1, keepdims=True) * SCORE_SCALE + shift
            highest = jnp.broadcast_to(highest, (ROWS, HEAD_DIM))
            if not initial:
                before = top[here, rows, :]
                highest = jnp.maximum(before, highest)
            base = highest - shift
            weights = [jnp.exp2(p * SCORE_SCALE - base) for p in parts]
            added = functools.reduce(jnp.add, weights)
            rounded = jnp.concatenate([w.astype(jnp.bfloat16) for w in weights], axis=1)
            update = jnp.dot(rounded, value_rows, preferred_element_type=jnp.float32)
            top[here, rows, :] = highest
            if initial:
                sums[here, rows, :] = added
                acc[here, rows, :] = update
            else:
                rescale = jnp.exp2(before - highest)
                sums[here, rows, :] = sums[here, rows, :] * rescale + added
                acc[here, rows, :] = acc[here, rows, :] * rescale + update

    def attend_slots(h, first, last):
        def one(slot, carry):
            @pl.when(pick(valid, slot) > 0)
            def _():
                @pl.when((slot <= XHI) | (slot >= NEAR))
                def _():
                    arrival(slot, h).wait_recv()

                attend(slot, h, False)

            return carry

        lax.fori_loop(first, last, one, 0)

    def attend_early(h):
        @pl.when(swapped == 1)
        def _():
            copies(MATE_Q, h).wait_recv()

        @pl.when(swapped == 0)
        def _():
            load_q(h).wait()

        attend(OWN, h, True)
        attend_slots(h, OTHER, LATE)

    def attend_late(h):
        attend_slots(h, LATE, SLOTS)
        here = lax.rem(h, 2)
        att[h, :, rows_of(half)] = (
            acc[here] / jnp.sum(sums[here], axis=1, keepdims=True)).astype(jnp.bfloat16)

    step = HEAD_DIM * 4

    def project(h, last):
        for c in range(0, width, step):
            columns = pl.ds(c, step)
            term = jnp.dot(att[h], wbuf[h, :, columns], preferred_element_type=jnp.float32)
            if last:
                out_ref[:, columns] = (total[:, columns] + term).astype(jnp.bfloat16)
            else:
                total[:, columns] += term

    pl.semaphore_wait(barrier, len(friends))

    give(0)
    send_own(0)
    give(1)
    total[...] = jnp.zeros_like(total)

    def turn(t, carry):
        @pl.when((t >= AGAIN) & (t < heads + AGAIN))
        def _():
            relay_again(t - AGAIN)

        @pl.when(t < heads)
        def _():
            relay(t)

        @pl.when(t + 1 < heads)
        def _():
            send_own(t + 1)

        @pl.when(t + 2 < heads)
        def _():
            give(t + 2)

        @pl.when(t == 1)
        def _():
            @pl.when(swapped == 0)
            def _():
                weight_piece().start()
                weight_piece(SIDE + 1, dev_head).start()

        @pl.when(t == 3)
        def _():
            weight_piece().wait_recv()
            for k in (1, 2, 3):
                weight_relay(k).start()

        @pl.when(t == 5)
        def _():
            for k in (1, 2, 3):
                weight_relay(k).wait_recv()
            weight_cross().start()

        @pl.when(t >= ATTEND)
        def _():
            relay_edge(t - ATTEND)
            attend_late(t - ATTEND)
            copies(TO_HEAD, t - ATTEND).start()

        @pl.when((t >= 1) & (t <= heads))
        def _():
            attend_early(t - 1)

        return carry

    lax.fori_loop(0, heads + ATTEND, turn, 0)
    load_w.wait()
    weight_cross().wait_recv()

    def finish(h, carry):
        copies(TO_HEAD, h).wait_recv()
        project(h, False)
        return carry

    lax.fori_loop(0, heads - 1, finish, 0)
    copies(TO_HEAD, heads - 1).wait_recv()
    project(heads - 1, True)

    def drain(h, carry):
        for kind in (TO_ZP, TO_ZM, RELAY_Z, TO_YDOWN, RELAY_YDOWN, TO_CORE, TO_HEAD):
            copies(kind, h).wait_send()

        @pl.when(swapped == 1)
        def _():
            copies(TO_MATE, h).wait_send()
            copies(MATE_Q, h).wait_send()

        @pl.when(ym != 1)
        def _():
            copies(LAST_YDOWN, h).wait_send()

        @pl.when(has_yup)
        def _():
            copies(TO_YUP, h).wait_send()
            copies(TO_EDGE2, h).wait_send()

        @pl.when(edge1_out)
        def _():
            copies(TO_EDGE1, h).wait_send()

        @pl.when(x > 0)
        def _():
            copies(TO_XDOWN, h).wait_send()

        @pl.when(x < SIDE - 1)
        def _():
            copies(TO_XUP, h).wait_send()

        @pl.when(gives_near)
        def _():
            near_copy(h, OWN).wait_send()

        return carry

    lax.fori_loop(0, heads, drain, 0)

    @pl.when(swapped == 0)
    def _():
        weight_piece().wait_send()
        weight_piece(SIDE + 1, dev_head).wait_send()

    for k in (1, 2, 3):
        weight_relay(k).wait_send()
    weight_cross().wait_send()


def body(queries, keys, values, out_weight, kv_list, kv_count):
    tokens, features = queries.shape
    heads = features // HEAD_DIM
    model = out_weight.shape[1]
    weight = out_weight.reshape(heads, HEAD_DIM, model)
    vmem = pl.BlockSpec(memory_space=pltpu.VMEM)
    smem = pl.BlockSpec(memory_space=pltpu.SMEM)
    anywhere = pl.BlockSpec(memory_space=pl.ANY)
    return pl.pallas_call(
        functools.partial(kernel, heads),
        out_shape=jax.ShapeDtypeStruct((tokens, model // 2), jnp.bfloat16),
        in_specs=[smem, smem, anywhere, anywhere, anywhere, anywhere],
        out_specs=vmem,
        scratch_shapes=[
            pltpu.VMEM((SLOTS + 1, heads, 2, tokens, HEAD_DIM), jnp.bfloat16),
            pltpu.VMEM((heads, tokens, HEAD_DIM), jnp.bfloat16),
            pltpu.VMEM((heads, tokens, 2 * HEAD_DIM), jnp.bfloat16),
            pltpu.VMEM((heads, 2 * HEAD_DIM, model // 2), jnp.bfloat16),
            pltpu.VMEM((tokens, model // 2), jnp.float32),
            pltpu.VMEM((2, tokens, HEAD_DIM), jnp.float32),
            pltpu.VMEM((2, tokens, HEAD_DIM), jnp.float32),
            pltpu.VMEM((2, tokens, HEAD_DIM), jnp.float32),
            pltpu.SemaphoreType.DMA((SENDS, heads)),
            pltpu.SemaphoreType.DMA((SLOTS, heads)),
            pltpu.SemaphoreType.DMA((heads,)),
            pltpu.SemaphoreType.DMA((heads,)),
            pltpu.SemaphoreType.DMA((heads,)),
            pltpu.SemaphoreType.DMA((heads, 3)),
            pltpu.SemaphoreType.DMA,
            pltpu.SemaphoreType.DMA((SIDE + 2,)),
            pltpu.SemaphoreType.DMA((SIDE + 2,)),
        ],
        compiler_params=pltpu.CompilerParams(
            collective_id=0, has_side_effects=True, vmem_limit_bytes=56 * 1024 * 1024),
    )(kv_list, kv_count, queries, keys, values, weight)


def solution(mesh):
    rows = P(("tm", "height"), "head")
    return jax.shard_map(
        body,
        mesh=mesh,
        in_specs=(rows, rows, rows, P("head", None), P(("tm", "height"), None),
                  P(("tm", "height"))),
        out_specs=rows,
        check_vma=False,
    )
```

```python
import functools

import jax
import jax.numpy as jnp
from jax import lax
from jax.experimental import pallas as pl
from jax.experimental.pallas import tpu as pltpu
from jax.sharding import PartitionSpec as P

HEAD_DIM = 128
SIDE = 4
SCORE_SCALE = HEAD_DIM ** (-0.5) * 1.4426950408889634
UNLISTED = -1e30
ROWS = 512
AGAIN, ATTEND = 1, 2

OWN, OTHER, XLO, XHI, YHI, ZP, ZM, ZOP, YOP, YLO, EDGE1, NEAR, EDGE2 = range(13)
LATE = YLO
SLOTS = 13
SOURCE = 13

(TO_ZP, TO_ZM, RELAY_Z, TO_MATE, MATE_Q, TO_YDOWN, RELAY_YDOWN, LAST_YDOWN, TO_YUP, TO_EDGE1,
 TO_EDGE2, TO_XDOWN, TO_XUP, TO_CORE, TO_NEAR, TO_HEAD) = range(16)
SENDS = 16


def kernel(heads, kv_list, kv_count, q_hbm, k_hbm, v_hbm, w_hbm, out_ref,
           kv, queries, att, wbuf, total, top, sums, acc,
           send, recv, recv_v, q_recv, att_recv, load, wload, wsend, wrecv):
    tm = lax.axis_index("tm")
    x = lax.axis_index("height")
    part = lax.axis_index("head")
    core = lax.rem(tm, 2)
    chip = lax.div(tm, 2)
    z = lax.rem(chip, SIDE)
    y = lax.div(chip, SIDE)
    far = lax.div(z, 2)
    sign = 1 - 2 * far
    ym = y * (1 - far) + (SIDE - 1 - y) * far
    zm = z * (1 - far) + (SIDE - 1 - z) * far

    def at(yy, zz, cc):
        return (yy * SIDE + zz) * 2 + cc

    swapped = 1 - lax.rem(z, 2)
    half = part * (1 - swapped) + (1 - part) * swapped
    ahead = 1 - 2 * half
    z_ahead = lax.rem(z + ahead + SIDE, SIDE)
    z_back = lax.rem(z - ahead + SIDE, SIDE)
    z_out = z_ahead * swapped + z_back * (1 - swapped)
    yup, ydown = lax.rem(y + sign + SIDE, SIDE), lax.rem(y - sign + SIDE, SIDE)
    dev_zp = (at(y, z_out, core), x, part * swapped + (1 - part) * (1 - swapped))
    dev_zm = (at(y, z_ahead, core), x, 1 - part)
    dev_relay = (at(y, z_out, core), x, 1 - part)
    dev_back = (at(y, z_back, core), x, 1 - part)
    dev_far = (at(y, z_ahead, core), x, part)
    dev_yup = (at(yup, z, core), x, part)
    dev_ydown = (at(ydown, z, core), x, part)
    dev_core = (at(y, z, 1 - core), x, part)
    dev_head = (tm, x, 1 - part)
    dev_beside = (at(y, lax.rem(z + part + (1 - part) * 3, SIDE), core), x, 1 - part)
    dev_x = [None] + [(tm, lax.rem(x + k, SIDE), part) for k in (1, 2, 3)]

    barrier = pltpu.get_barrier_semaphore()
    friends = [dev_zm, dev_back, dev_far, dev_yup, dev_ydown, dev_core, dev_head] + dev_x[1:]
    for friend in friends:
        pl.semaphore_signal(barrier, inc=1, device_id=friend, device_id_type=pl.DeviceIdType.MESH)

    source = OWN + (SOURCE - OWN) * swapped

    def columns_of(h):
        return pl.ds(pl.multiple_of(h * HEAD_DIM, HEAD_DIM), HEAD_DIM)

    def loads(h):
        return (pltpu.make_async_copy(k_hbm.at[:, columns_of(h)], kv.at[source, h, 0], load.at[h, 0]),
                pltpu.make_async_copy(v_hbm.at[:, columns_of(h)], kv.at[source, h, 1], load.at[h, 1]))

    def load_q(h):
        return pltpu.make_async_copy(q_hbm.at[:, columns_of(h)], queries.at[h], load.at[h, 2])

    for h in range(heads):
        for copy in loads(h):
            copy.start()

        @pl.when(swapped == 0)
        def _():
            load_q(h).start()

    width = w_hbm.shape[2] // 2

    def rows_of(heads_half):
        return pl.ds(pl.multiple_of(heads_half * HEAD_DIM, HEAD_DIM), HEAD_DIM)

    mine = pl.ds(pl.multiple_of(part * width, HEAD_DIM), width)
    load_w = pltpu.make_async_copy(w_hbm.at[:, :, mine], wbuf.at[:, rows_of(part), :], wload)
    load_w.start()

    has_yup = ym < SIDE - 1
    has_ydown = ym > 0
    edge1_out = (zm == 0) & has_yup
    edge1_in = (zm == 0) & has_ydown
    has_near = ((core == 0) & (chip > 0)) | ((core == 1) & (chip < SIDE * SIDE - 1))
    gives_near = ((core == 1) & (chip > 0)) | ((core == 0) & (chip < SIDE * SIDE - 1))
    near_at_edge = ((core == 1) & (z == 0)) | ((core == 0) & (z == SIDE - 1))
    half_is_first = 1 - half
    slot_after = ZM + (ZP - ZM) * half_is_first
    slot_before = ZP + (ZM - ZP) * half_is_first
    near_slot = slot_after * (1 - core) + slot_before * core
    edge_slot = slot_before * (1 - far) + slot_after * far
    relay_slot = ZP + (ZM - ZP) * swapped
    late_slot = ZM + (ZP - ZM) * swapped

    def remote(kind, h, src, dst, sem, device):
        return pltpu.make_async_remote_copy(
            src_ref=src, dst_ref=dst, send_sem=send.at[kind, h], recv_sem=sem,
            device_id=device, device_id_type=pl.DeviceIdType.MESH)

    def pair(kind, h, source, slot, device):
        return remote(kind, h, kv.at[source, h], kv.at[slot, h], recv.at[slot, h], device)

    def arrival(slot, h, device=None):
        return pair(TO_CORE, h, slot, slot, dev_core)

    def copies(kind, h):
        if kind == TO_ZP:
            return pair(kind, h, source, ZP, dev_zp)
        if kind == TO_ZM:
            return pair(kind, h, OWN, ZM, dev_zm)
        if kind == RELAY_Z:
            return pair(kind, h, relay_slot, ZOP, dev_relay)
        if kind == TO_MATE:
            return pair(kind, h, SOURCE, OWN, dev_head)
        if kind == MATE_Q:
            return remote(kind, h, q_hbm.at[:, columns_of(h)], queries.at[h], q_recv.at[h], dev_head)
        if kind == TO_YDOWN:
            return pair(kind, h, OWN, YHI, dev_ydown)
        if kind == RELAY_YDOWN:
            return pair(kind, h, YHI, YOP, dev_ydown)
        if kind == TO_YUP:
            return remote(kind, h, kv.at[OWN, h, 0], kv.at[YLO, h, 0], recv.at[YLO, h], dev_yup)
        if kind == LAST_YDOWN:
            return remote(kind, h, kv.at[YOP, h, 1], kv.at[YLO, h, 1], recv_v.at[h], dev_ydown)
        if kind == TO_EDGE1:
            return pair(kind, h, edge_slot, EDGE1, dev_yup)
        if kind == TO_EDGE2:
            return pair(kind, h, ZOP, EDGE2, dev_yup)
        if kind == TO_XDOWN:
            return pair(kind, h, OWN, XHI, dev_x[3])
        if kind == TO_XUP:
            return pair(kind, h, OWN, XLO, dev_x[1])
        if kind == TO_CORE:
            return pair(kind, h, OWN, OTHER, dev_core)
        if kind == TO_HEAD:
            piece = att.at[h, :, rows_of(half)]
            return remote(kind, h, piece, piece, att_recv.at[h], dev_head)

    def near_copy(h, slot):
        return pair(TO_NEAR, h, slot, NEAR, dev_core)

    def give(h):
        for copy in loads(h):
            copy.wait()

        @pl.when(swapped == 1)
        def _():
            copies(TO_MATE, h).start()

    def send_own(h):
        copies(TO_ZP, h).start()

        @pl.when(swapped == 1)
        def _():
            arrival(OWN, h).wait_recv()

        for kind in (TO_ZM, TO_YDOWN):
            copies(kind, h).start()

        @pl.when(has_yup)
        def _():
            copies(TO_YUP, h).start()

        @pl.when(x > 0)
        def _():
            copies(TO_XDOWN, h).start()

        @pl.when(x < SIDE - 1)
        def _():
            copies(TO_XUP, h).start()

        copies(TO_CORE, h).start()

    def relay(h):
        arrival(relay_slot, h).wait_recv()
        copies(RELAY_Z, h).start()
        arrival(YHI, h).wait_recv()
        copies(RELAY_YDOWN, h).start()

        @pl.when(swapped == 1)
        def _():
            copies(MATE_Q, h).start()

    def relay_again(h):
        arrival(late_slot, h).wait_recv()

        @pl.when(edge1_out)
        def _():
            copies(TO_EDGE1, h).start()

        @pl.when(gives_near & jnp.logical_not(near_at_edge))
        def _():
            near_copy(h, near_slot).start()

        arrival(YOP, h).wait_recv()

        @pl.when(ym != 1)
        def _():
            copies(LAST_YDOWN, h).start()

        arrival(ZOP, h).wait_recv()

        @pl.when(has_yup)
        def _():
            copies(TO_EDGE2, h).start()

    def relay_edge(h):
        @pl.when(has_ydown)
        def _():
            copies(TO_YUP, h).wait_recv()
            copies(LAST_YDOWN, h).wait_recv()

        @pl.when(edge1_in)
        def _():
            arrival(EDGE1, h).wait_recv()

        @pl.when(gives_near & near_at_edge)
        def _():
            near_copy(h, EDGE1).start()

    group = heads // 2
    chunk = width // SIDE

    def weight_piece(sem=0, device=dev_beside):
        return pltpu.make_async_remote_copy(
            src_ref=w_hbm.at[pl.ds(core * group, group), :,
                             pl.ds(pl.multiple_of((1 - part) * width + x * chunk, HEAD_DIM), chunk)],
            dst_ref=wbuf.at[pl.ds(core * group, group), rows_of(part),
                            pl.ds(pl.multiple_of(x * chunk, HEAD_DIM), chunk)],
            send_sem=wsend.at[sem], recv_sem=wrecv.at[0],
            device_id=device, device_id_type=pl.DeviceIdType.MESH)

    def weight_relay(k):
        piece = wbuf.at[pl.ds(core * group, group), rows_of(1 - part),
                        pl.ds(pl.multiple_of(x * chunk, HEAD_DIM), chunk)]
        return pltpu.make_async_remote_copy(
            src_ref=piece, dst_ref=piece, send_sem=wsend.at[k], recv_sem=wrecv.at[k],
            device_id=dev_x[k], device_id_type=pl.DeviceIdType.MESH)

    def weight_cross():
        piece = wbuf.at[pl.ds(core * group, group), rows_of(1 - part), :]
        return pltpu.make_async_remote_copy(
            src_ref=piece, dst_ref=piece, send_sem=wsend.at[SIDE], recv_sem=wrecv.at[SIDE],
            device_id=dev_core, device_id_type=pl.DeviceIdType.MESH)

    frame = tm
    bands = SIDE
    always = 1 + 0 * z
    valid = [always, always, x > 0, x < SIDE - 1, has_yup, (z + ahead >= 0) & (z + ahead < SIDE),
             (z - ahead >= 0) & (z - ahead < SIDE), always, always, has_ydown, edge1_in, has_near,
             has_ydown]
    valid = [jnp.int32(v) if isinstance(v, int) else v.astype(jnp.int32) for v in valid]
    block_of = [
        frame * bands + x,
        (frame + 1 - 2 * core) * bands + x,
        frame * bands + x - 1,
        frame * bands + x + 1,
        (frame + 8 * sign) * bands + x,
        (frame + 2 * ahead) * bands + x,
        (frame - 2 * ahead) * bands + x,
        at(y, lax.rem(z + 2, SIDE), core) * bands + x,
        at(lax.rem(y + 2, SIDE), z, core) * bands + x,
        (frame - 8 * sign) * bands + x,
        (frame - 2 * sign) * bands + x,
        (frame - 1 + 2 * core) * bands + x,
        (frame - 4 * sign) * bands + x,
    ]

    def pick(values, i):
        return sum((i == k).astype(jnp.int32) * values[k] for k in range(SLOTS))

    def attend(slot, h, initial):
        if initial:
            shift = jnp.float32(0)
        else:
            block = pick(block_of, slot)
            hits = sum(((kv_list[0, j] == block) & (j < kv_count[0])).astype(jnp.int32)
                       for j in range(kv_list.shape[1]))
            shift = jnp.where(hits > 0, jnp.float32(0), jnp.float32(UNLISTED))
        here = lax.rem(h, 2)
        key_rows = kv[slot, h, 0]
        value_rows = kv[slot, h, 1]
        count = key_rows.shape[0] // HEAD_DIM
        for r in range(0, queries.shape[1], ROWS):
            rows = pl.ds(r, ROWS)
            scores = lax.dot_general(queries[h, rows, :], key_rows, (((1,), (1,)), ((), ())),
                                     preferred_element_type=jnp.float32)
            parts = [scores[:, i * HEAD_DIM:(i + 1) * HEAD_DIM] for i in range(count)]
            highest = functools.reduce(jnp.maximum, parts)
            highest = jnp.max(highest, axis=1, keepdims=True) * SCORE_SCALE + shift
            highest = jnp.broadcast_to(highest, (ROWS, HEAD_DIM))
            if not initial:
                before = top[here, rows, :]
                highest = jnp.maximum(before, highest)
            base = highest - shift
            weights = [jnp.exp2(p * SCORE_SCALE - base) for p in parts]
            added = functools.reduce(jnp.add, weights)
            rounded = jnp.concatenate([w.astype(jnp.bfloat16) for w in weights], axis=1)
            update = jnp.dot(rounded, value_rows, preferred_element_type=jnp.float32)
            top[here, rows, :] = highest
            if initial:
                sums[here, rows, :] = added
                acc[here, rows, :] = update
            else:
                rescale = jnp.exp2(before - highest)
                sums[here, rows, :] = sums[here, rows, :] * rescale + added
                acc[here, rows, :] = acc[here, rows, :] * rescale + update

    def attend_slots(h, first, last):
        def one(slot, carry):
            @pl.when(pick(valid, slot) > 0)
            def _():
                @pl.when((slot <= XHI) | (slot >= NEAR))
                def _():
                    arrival(slot, h).wait_recv()

                attend(slot, h, False)

            return carry

        lax.fori_loop(first, last, one, 0)

    def attend_early(h):
        @pl.when(swapped == 1)
        def _():
            copies(MATE_Q, h).wait_recv()

        @pl.when(swapped == 0)
        def _():
            load_q(h).wait()

        attend(OWN, h, True)
        attend_slots(h, OTHER, LATE)

    def attend_late(h):
        attend_slots(h, LATE, SLOTS)
        here = lax.rem(h, 2)
        att[h, :, rows_of(half)] = (
            acc[here] / jnp.sum(sums[here], axis=1, keepdims=True)).astype(jnp.bfloat16)

    step = HEAD_DIM * 4

    def project(h, last):
        for c in range(0, width, step):
            columns = pl.ds(c, step)
            term = jnp.dot(att[h], wbuf[h, :, columns], preferred_element_type=jnp.float32)
            if last:
                out_ref[:, columns] = (total[:, columns] + term).astype(jnp.bfloat16)
            else:
                total[:, columns] += term

    pl.semaphore_wait(barrier, len(friends))

    give(0)
    send_own(0)
    give(1)
    total[...] = jnp.zeros_like(total)

    def turn(t, carry):
        @pl.when((t >= AGAIN) & (t < heads + AGAIN))
        def _():
            relay_again(t - AGAIN)

        @pl.when(t < heads)
        def _():
            relay(t)

        @pl.when(t + 1 < heads)
        def _():
            send_own(t + 1)

        @pl.when(t + 2 < heads)
        def _():
            give(t + 2)

        @pl.when(t == 1)
        def _():
            @pl.when(swapped == 0)
            def _():
                weight_piece().start()
                weight_piece(SIDE + 1, dev_head).start()

        @pl.when(t == 3)
        def _():
            weight_piece().wait_recv()
            for k in (1, 2, 3):
                weight_relay(k).start()

        @pl.when(t == 5)
        def _():
            for k in (1, 2, 3):
                weight_relay(k).wait_recv()
            weight_cross().start()

        @pl.when(t >= ATTEND)
        def _():
            relay_edge(t - ATTEND)
            attend_late(t - ATTEND)
            copies(TO_HEAD, t - ATTEND).start()

        @pl.when((t >= 1) & (t <= heads))
        def _():
            attend_early(t - 1)

        return carry

    lax.fori_loop(0, heads + ATTEND, turn, 0)
    load_w.wait()
    weight_cross().wait_recv()

    def finish(h, carry):
        copies(TO_HEAD, h).wait_recv()
        project(h, False)
        return carry

    lax.fori_loop(0, heads - 1, finish, 0)
    copies(TO_HEAD, heads - 1).wait_recv()
    project(heads - 1, True)

    def drain(h, carry):
        for kind in (TO_ZP, TO_ZM, RELAY_Z, TO_YDOWN, RELAY_YDOWN, TO_CORE, TO_HEAD):
            copies(kind, h).wait_send()

        @pl.when(swapped == 1)
        def _():
            copies(TO_MATE, h).wait_send()
            copies(MATE_Q, h).wait_send()

        @pl.when(ym != 1)
        def _():
            copies(LAST_YDOWN, h).wait_send()

        @pl.when(has_yup)
        def _():
            copies(TO_YUP, h).wait_send()
            copies(TO_EDGE2, h).wait_send()

        @pl.when(edge1_out)
        def _():
            copies(TO_EDGE1, h).wait_send()

        @pl.when(x > 0)
        def _():
            copies(TO_XDOWN, h).wait_send()

        @pl.when(x < SIDE - 1)
        def _():
            copies(TO_XUP, h).wait_send()

        @pl.when(gives_near)
        def _():
            near_copy(h, OWN).wait_send()

        return carry

    lax.fori_loop(0, heads, drain, 0)

    @pl.when(swapped == 0)
    def _():
        weight_piece().wait_send()
        weight_piece(SIDE + 1, dev_head).wait_send()

    for k in (1, 2, 3):
        weight_relay(k).wait_send()
    weight_cross().wait_send()


def body(queries, keys, values, out_weight, kv_list, kv_count):
    tokens, features = queries.shape
    heads = features // HEAD_DIM
    model = out_weight.shape[1]
    weight = out_weight.reshape(heads, HEAD_DIM, model)
    vmem = pl.BlockSpec(memory_space=pltpu.VMEM)
    smem = pl.BlockSpec(memory_space=pltpu.SMEM)
    anywhere = pl.BlockSpec(memory_space=pl.ANY)
    return pl.pallas_call(
        functools.partial(kernel, heads),
        out_shape=jax.ShapeDtypeStruct((tokens, model // 2), jnp.bfloat16),
        in_specs=[smem, smem, anywhere, anywhere, anywhere, anywhere],
        out_specs=vmem,
        scratch_shapes=[
            pltpu.VMEM((SLOTS + 1, heads, 2, tokens, HEAD_DIM), jnp.bfloat16),
            pltpu.VMEM((heads, tokens, HEAD_DIM), jnp.bfloat16),
            pltpu.VMEM((heads, tokens, 2 * HEAD_DIM), jnp.bfloat16),
            pltpu.VMEM((heads, 2 * HEAD_DIM, model // 2), jnp.bfloat16),
            pltpu.VMEM((tokens, model // 2), jnp.float32),
            pltpu.VMEM((2, tokens, HEAD_DIM), jnp.float32),
            pltpu.VMEM((2, tokens, HEAD_DIM), jnp.float32),
            pltpu.VMEM((2, tokens, HEAD_DIM), jnp.float32),
            pltpu.SemaphoreType.DMA((SENDS, heads)),
            pltpu.SemaphoreType.DMA((SLOTS, heads)),
            pltpu.SemaphoreType.DMA((heads,)),
            pltpu.SemaphoreType.DMA((heads,)),
            pltpu.SemaphoreType.DMA((heads,)),
            pltpu.SemaphoreType.DMA((heads, 3)),
            pltpu.SemaphoreType.DMA,
            pltpu.SemaphoreType.DMA((SIDE + 2,)),
            pltpu.SemaphoreType.DMA((SIDE + 2,)),
        ],
        compiler_params=pltpu.CompilerParams(
            collective_id=0, has_side_effects=True, vmem_limit_bytes=56 * 1024 * 1024),
    )(kv_list, kv_count, queries, keys, values, weight)


def solution(mesh):
    rows = P(("tm", "height"), "head")
    return jax.shard_map(
        body,
        mesh=mesh,
        in_specs=(rows, rows, rows, P("head", None), P(("tm", "height"), None),
                  P(("tm", "height"))),
        out_specs=rows,
        check_vma=False,
    )
```
